32 devices in a mesh: dp: 8 (over z, x), grp: 4 (over y, core).
Axes of the slice: x: 2, y: 2, z: 4, core: 2. Of those that a mesh axis runs over, the one named last changes fastest.
Arguments:
- images: bfloat16 [16384, 128, 128], P(('dp', 'grp')), may hold values from -6 to 6
- shifts: int32 [16384, 2], P(('dp', 'grp')), may hold values from -16 to 16
- class_ids: int32 [16384], P(('dp', 'grp')), may hold values from 0 to 255
- next_block: bfloat16 [1024, 2, 4096], P('grp'), may hold values from -6 to 6
Outputs:
- averages: float32 [256, 2, 4096], P(('dp', 'grp'))
- scores: float32 [256, 1024], P('dp', 'grp')
The draws below stay inside these ranges and needn't reach their ends.
All inputs are finite; a program needn't handle non-finite values.
Results may differ from the reference program's by a relative error of at most 0.014.
Values may be sent and summed in bfloat16 or wider, within the bound.
No kernel may reach another device: no remote copies, remote signals or barrier semaphores. Data moves between devices by JAX's collectives and lax.ppermute only.
A program may use at most 128 MiB of HBM per device.

```python
import math
import jax
import jax.numpy as jnp
import numpy as np
from jax import lax

PIX = 128
BAND = 64
CLASSES = 256
IMG_DEV = 512
IMAGES = 16384
NEXT = 1024


def with_ends(array, rng, smallest, top_value):
    dims = array.shape
    index_at = [jax.random.randint(jax.random.fold_in(rng, axis), (), 0, dims[axis]) for axis in range(len(dims))]
    array = array.at[tuple(index_at)].set(smallest)
    longest = dims.index(max(dims))
    index_at[longest] = (index_at[longest] + 1) % dims[longest]
    return array.at[tuple(index_at)].set(top_value)


def steps_of(rng, dims, shards, least, largest):
    def one(position, shards_of):
        heights = jax.random.uniform(jax.random.fold_in(jax.random.fold_in(rng, 6), position), (shards_of,), jnp.float32, least / len(shards), largest / len(shards))
        return jnp.repeat(jnp.exp(heights), dims[position] // shards_of).reshape((-1,) + (1,) * (len(dims) - position - 1))

    factor_of = one(*shards[0])
    for cut in shards[1:]:
        factor_of = factor_of * one(*cut)
    return factor_of


def cumulative_ranks(amount, lean):
    weights = [(1 << 20) // math.isqrt(standing ** lean) + 1 for standing in range(1, amount + 1)]
    spread = 1 + sum(weights) // (1 << 30)
    return np.cumsum(np.array([max(1, weight // spread) for weight in weights]))


def ranked(stream_key, extent, count, skew):
    listing = cumulative_ranks(count, skew)
    lot = jax.random.randint(jax.random.fold_in(stream_key, 1), extent, 0, int(listing[count - 1]))
    rank = jnp.searchsorted(jnp.asarray(listing, jnp.int32), lot, side="right")
    return jax.random.permutation(jax.random.fold_in(stream_key, 2), count)[rank].astype(jnp.int32)


def normal_values(key, dims, spread, reach, pieces=(), held_as=jnp.bfloat16):
    entries = spread * jax.random.normal(key, dims, jnp.float32)
    if pieces:
        entries = entries * steps_of(key, dims, pieces, -0.22, 0.18)
    return jnp.clip(entries, -reach, reach).astype(held_as)


def setup_inputs(seed: int = 0) -> dict:
    streams_of = jax.random.split(jax.random.key(seed), 5)
    return {
        "images": normal_values(streams_of[0], (IMAGES, PIX, PIX), 1.0, 6.0, ((0, 32),)),
        "shifts": with_ends(jax.random.randint(streams_of[1], (IMAGES, 2), -(PIX // 8), PIX // 8 + 1), jax.random.fold_in(streams_of[1], 1), -(PIX // 8), (PIX // 8 + 1) - 1).astype(jnp.int32),
        "class_ids": with_ends(ranked(streams_of[2], (IMAGES,), CLASSES, 1), jax.random.fold_in(streams_of[2], 3), 0, CLASSES - 1).astype(jnp.int32),
        "next_block": normal_values(streams_of[3], (NEXT, 2, BAND * BAND), 1.0, 6.0, ((0, 4),)),
    }


ridge = 4.0

def dft_tables():
    positions = jnp.arange(PIX, dtype=jnp.int32)
    signed_freq = jnp.arange(BAND, dtype=jnp.int32) - BAND // 2
    residue = positions[:, None] * signed_freq[None, :] % PIX
    phase_angle = residue.astype(jnp.float32) * (2.0 * math.pi / PIX)
    scaling = 1.0 / math.sqrt(PIX)
    cosine = (jnp.cos(phase_angle) * scaling).astype(jnp.bfloat16)
    sine = (jnp.sin(phase_angle) * scaling).astype(jnp.bfloat16)
    return (jnp.concatenate([cosine, sine], axis=1), signed_freq)

def band_filter(signed_freq):
    squared = signed_freq.astype(jnp.float32) ** 2
    radius = squared[:, None] + squared[None, :]
    return jnp.exp(-radius / (BAND * BAND / 2.0)).reshape(BAND * BAND)

def shifted_transform(block_imgs, block_shifts, tables, signed_freq):
    num_img = block_imgs.shape[0]
    column_section = jnp.einsum('iyx,xm->iym', block_imgs.astype(jnp.float32), tables.astype(jnp.float32)).astype(jnp.bfloat16)
    row_section = jnp.einsum('yt,iym->itm', tables.astype(jnp.float32), column_section.astype(jnp.float32))
    cos_cos = row_section[:, :BAND, :BAND]
    cos_sin = row_section[:, :BAND, BAND:]
    sin_cos = row_section[:, BAND:, :BAND]
    sin_sin = row_section[:, BAND:, BAND:]
    four_real = cos_cos - sin_sin
    four_imag = -(sin_cos + cos_sin)
    shift_x = block_shifts[:, 0][:, None, None]
    shift_y = block_shifts[:, 1][:, None, None]
    residue = (signed_freq[None, :, None] * shift_y + signed_freq[None, None, :] * shift_x) % PIX
    phase_angle = residue.astype(jnp.float32) * (2.0 * math.pi / PIX)
    ramp_cos = jnp.cos(phase_angle)
    ramp_sin = jnp.sin(phase_angle)
    moved_real = four_real * ramp_cos + four_imag * ramp_sin
    moved_imag = four_imag * ramp_cos - four_real * ramp_sin
    return jnp.stack([moved_real, moved_imag], axis=1).reshape(num_img, 2 * BAND * BAND).astype(jnp.bfloat16)

def reference(images, shifts, class_ids, next_block):
    tables, signed_freq = dft_tables()
    blocks = IMAGES // IMG_DEV
    stacked = (images.reshape(blocks, IMG_DEV, PIX, PIX), shifts.reshape(blocks, IMG_DEV, 2), class_ids.reshape(blocks, IMG_DEV))

    def accumulate(running, item):
        moved = shifted_transform(item[0], item[1], tables, signed_freq)
        added = jax.ops.segment_sum(moved.astype(jnp.float32), item[2], num_segments=CLASSES)
        return (running + added, None)
    class_sum, _ = lax.scan(accumulate, jnp.zeros((CLASSES, 2 * BAND * BAND), jnp.float32), stacked)
    members = jax.ops.segment_sum(jnp.ones((IMAGES,), jnp.float32), class_ids, num_segments=CLASSES)
    averages = class_sum.reshape(CLASSES, 2, BAND * BAND) * band_filter(signed_freq)[None, None, :] / (members + ridge)[:, None, None]
    references = averages.astype(jnp.bfloat16)
    energy = lax.optimization_barrier(jnp.sum(jnp.square(references.astype(jnp.float32)), axis=(1, 2)))
    inner_prod = jnp.dot(references.reshape(CLASSES, 2 * BAND * BAND), next_block.reshape(NEXT, 2 * BAND * BAND).T, preferred_element_type=jnp.float32)
    scores = (inner_prod - 0.5 * energy[:, None]) / BAND
    return (averages, scores)
```

```python
import functools
import math

import jax
import jax.numpy as jnp
import ml_dtypes
import numpy as np
from jax import lax
from jax.experimental import pallas as pl
from jax.experimental.pallas import tpu as pltpu
from jax.sharding import PartitionSpec as P

PIX = 128
BAND = 64
CLASSES = 256
HALF = BAND // 2
RIDGE = 4.0
REACH = 16
SLAB = PIX + 2 * REACH
TILE = 8
PACK = 16
DIGITS = 4
CHUNK = 32
UNROLL = 8
MIB = 1 << 20


def basis():
    position = np.arange(PIX)
    freq = np.concatenate([np.arange(HALF + 1), np.arange(1, HALF + 1)])
    angle = (position[:, None] * freq[None, :] % PIX) * (2.0 * math.pi / PIX)
    is_cos = np.arange(BAND + 1) <= HALF
    table = np.where(is_cos[None, :], np.cos(angle), np.sin(angle)) / math.sqrt(PIX)
    return table.astype(np.float32).astype(ml_dtypes.bfloat16)


def column_table(pairs):
    table = basis()
    out = np.zeros((2 * PIX, 2 * PIX), ml_dtypes.bfloat16)
    for side in range(2):
        rows = slice(side * PIX, (side + 1) * PIX)
        out[rows, side * BAND : (side + 1) * BAND] = table[:, :BAND]
        out[rows, PIX + side * pairs] = table[:, BAND]
    return out


def row_table():
    out = np.zeros((5 * PACK, PIX), ml_dtypes.bfloat16)
    out[: BAND + 1] = basis().T
    return out


def expand_table():
    out = np.zeros((PIX, 2 * PIX), np.float32)
    for at in range(BAND):
        k = at - HALF
        for copy in range(2):
            out[abs(k), copy * BAND + at] = 1.0
            if k:
                row = BAND if abs(k) == HALF else HALF + abs(k)
                out[row, PIX + copy * BAND + at] = math.copysign(1.0, k)
    return out


def filter_table():
    squared = (np.arange(BAND, dtype=np.float32) - HALF) ** 2
    radius = squared[:, None] + squared[None, :]
    return np.exp(-radius / (BAND * BAND / 2.0)).reshape(BAND // 2, 2 * BAND).astype(np.float32)


def owner_of(me, near, far, other, groups):
    dp, grp = me[0], me[1]
    there_dp = dp ^ ((far << 1) | (near & 1))
    there_grp = grp ^ (((near >> 1) << 1) | other)
    return there_dp * groups + there_grp


def sums_kernel(
    me, ids, shifts, ids_rows, images, col, row, send, keep, held, acc, sems, *, groups, own
):
    count = images.shape[0]
    chunks = count // CHUNK
    pairs = own // 2
    nears, fars = send.shape[0], send.shape[1]

    def fetch(k):
        span = pl.ds(pl.multiple_of(k * CHUNK, CHUNK), CHUNK)
        return pltpu.make_async_copy(images.at[span], held.at[span], sems.at[k])

    for k in range(chunks):
        fetch(k).start()
    acc[...] = jnp.zeros_like(acc)

    def add_chunk(k, _):
        fetch(k).wait()

        def add_some(s, _):
            for u in range(UNROLL):
                i = k * CHUNK + s * UNROLL + u
                dx = shifts[0, i]
                at = ids[i] * SLAB + REACH + shifts[1, i]
                turned = pltpu.roll(
                    held[i].astype(jnp.float32), jnp.where(dx < 0, dx + PIX, dx), 1
                )
                acc[pl.ds(at, PIX), :] = acc[pl.ds(at, PIX), :] + turned
            return 0

        return lax.fori_loop(0, CHUNK // UNROLL, add_some, 0)

    lax.fori_loop(0, chunks, add_chunk, 0)

    lane = lax.broadcasted_iota(jnp.int32, (TILE, PIX), 1)
    sub = lax.broadcasted_iota(jnp.int32, (TILE, PIX), 0)

    def folded(c):
        at = pl.multiple_of(c * SLAB, TILE)
        head = acc[pl.ds(at + REACH, REACH), :] + acc[pl.ds(at + PIX + REACH, REACH), :]
        mid = acc[pl.ds(at + 2 * REACH, PIX - 2 * REACH), :]
        tail = acc[pl.ds(at + PIX, REACH), :] + acc[pl.ds(at, REACH), :]
        return jnp.concatenate([head, mid, tail], axis=0).astype(jnp.bfloat16)

    def transform(owner, out):
        stacked = jnp.concatenate(
            [
                jnp.concatenate([folded(owner * own + j), folded(owner * own + j + pairs)], axis=1)
                for j in range(pairs)
            ],
            axis=0,
        )
        section = jnp.dot(stacked, col[...], preferred_element_type=jnp.float32).astype(
            jnp.bfloat16
        )
        extra = None
        edge = []
        for j in range(pairs):
            both = jnp.dot(
                row[...], section[j * PIX : (j + 1) * PIX], preferred_element_type=jnp.float32
            )
            out[j * BAND : (j + 1) * BAND, :] = both[:BAND, :PIX].astype(jnp.bfloat16)
            edge.append(both[BAND : BAND + 1, :PIX])
            last = both[:, PIX:]
            last = pltpu.roll(last, j, 1) if j else last
            extra = last if extra is None else extra + last
        extra = jnp.concatenate(
            [extra, jnp.zeros((PIX - extra.shape[0], PIX), jnp.float32)], axis=0
        ).T[:TILE]
        hits = jnp.zeros((TILE, PIX), jnp.float32)
        for r in range(ids_rows.shape[0]):
            hits += (ids_rows[r : r + 1, :] == owner * own + sub).astype(jnp.float32)
        rest = jnp.sum(hits, axis=1, keepdims=True)
        for d in range(DIGITS):
            upper = jnp.floor(rest * 0.125) if d < DIGITS - 1 else jnp.zeros_like(rest)
            extra = jnp.where(lane == BAND + 1 + d, rest - 8.0 * upper, extra)
            rest = upper
        edge.append(jnp.zeros((TILE - pairs, PIX), jnp.float32))
        out[pairs * BAND :, :] = jnp.concatenate([*edge, extra], axis=0).astype(jnp.bfloat16)

    def one(n, _):
        near, far = n // fars, n % fars
        transform(owner_of(me, near, far, 1, groups), send.at[near, far])
        transform(owner_of(me, near, far, 0, groups), keep.at[near, far])
        return 0

    lax.fori_loop(0, nears * fars, one, 0)


def averages_kernel(*refs, own, parts):
    pieces, (expand, taper, real, imag, rounded, wide, rows) = refs[:parts], refs[parts:]
    pairs = own // 2
    total = pieces[0][...].astype(jnp.float32)
    for piece in pieces[1:]:
        total += piece[...].astype(jnp.float32)
    main, ends = total[: pairs * BAND], total[pairs * BAND :]
    if own < TILE:
        wide[...] = jnp.zeros_like(wide)
    wide[: pairs * BAND, :] = main
    wide[pairs * BAND : 2 * pairs * BAND, :] = pltpu.roll(main, BAND, 1)
    extra = ends[TILE:]
    lane = lax.broadcasted_iota(jnp.int32, (TILE, PIX), 1)
    for t in range(BAND + 1):
        if t < BAND:
            line = wide[pl.ds(t, TILE, stride=BAND), :]
        else:
            edge = ends[:pairs]
            line = jnp.concatenate([edge, pltpu.roll(ends[:TILE], BAND, 1)[:pairs]], axis=0)
            if own < TILE:
                line = jnp.concatenate([line, jnp.zeros((TILE - own, PIX), jnp.float32)], axis=0)
        line = jnp.where(
            lane < BAND, line, jnp.where(lane == BAND, extra[:, t : t + 1], 0.0)
        )
        rows[t * TILE : (t + 1) * TILE, :] = line
    spread = jnp.dot(
        rows[...], expand[...], preferred_element_type=jnp.float32, precision=lax.Precision.HIGHEST
    )

    def cos_part(t):
        return spread[t * TILE : (t + 1) * TILE, :PIX]

    def sin_part(t):
        return spread[t * TILE : (t + 1) * TILE, PIX:]

    members = jnp.zeros((TILE, 1), jnp.float32)
    for d in range(DIGITS):
        members += extra[:, BAND + 1 + d : BAND + 2 + d] * float(8**d)
    weight = members + RIDGE

    def at_frequency(k):
        c = abs(k)
        if k == 0:
            return cos_part(0), -sin_part(0)
        s = BAND if c == HALF else HALF + c
        if k > 0:
            return cos_part(c) - sin_part(s), -(cos_part(s) + sin_part(c))
        return cos_part(c) + sin_part(s), cos_part(s) - sin_part(c)

    for u in range(BAND // 2):
        even, odd = at_frequency(2 * u - HALF), at_frequency(2 * u + 1 - HALF)
        span = slice(u * PIX, (u + 1) * PIX)
        for part, out in ((0, real), (1, imag)):
            value = jnp.where(lane < BAND, even[part], odd[part]) * taper[u : u + 1, :] / weight
            out[:, span] = value
            at = part * BAND * BAND + u * PIX
            rounded[:, at : at + PIX] = value.astype(jnp.bfloat16)


def scores_kernel(me, *refs, own, groups):
    pieces, (block, out) = refs[:groups], refs[groups:]
    held = jnp.concatenate([piece[:own] for piece in pieces], axis=0)
    inner = lax.dot_general(
        held, block[...], (((1,), (1,)), ((), ())), preferred_element_type=jnp.float32
    )
    energy = jnp.sum(jnp.square(held.astype(jnp.float32)), axis=1, keepdims=True)
    result = (inner - 0.5 * energy) / BAND
    for k in range(groups):
        at = (me[1] ^ k) * own
        if own % TILE == 0:
            out[pl.ds(pl.multiple_of(at, TILE), own), :] = result[k * own : (k + 1) * own]
        else:
            for j in range(own):
                out[pl.ds(at + j, 1), :] = result[k * own + j : k * own + j + 1]


def swap(array, axis, flip):
    size = lax.axis_size(axis)
    return lax.ppermute(array, axis, [(i, i ^ flip) for i in range(size)])


def hop(array, near, groups):
    both = lax.axis_size("dp") * groups
    return lax.ppermute(
        array,
        ("dp", "grp"),
        [(i, i ^ ((near & 1) * groups | (near >> 1) * 2)) for i in range(both)],
    )


def body(images, shifts, class_ids, next_block):
    dp_count, groups = lax.axis_size("dp"), lax.axis_size("grp")
    own = CLASSES // (dp_count * groups)
    pairs = own // 2
    count = images.shape[0]
    nears, fars = groups, dp_count // 2
    block_rows = pairs * BAND + PACK
    me = jnp.stack([lax.axis_index("dp"), lax.axis_index("grp")]).astype(jnp.int32)
    smem = pl.BlockSpec(memory_space=pltpu.SMEM)
    vmem = pl.BlockSpec(memory_space=pltpu.VMEM)
    hbm = pl.BlockSpec(memory_space=pl.ANY)
    partial = jax.ShapeDtypeStruct((nears, fars, block_rows, PIX), jnp.bfloat16)
    send, keep = pl.pallas_call(
        functools.partial(sums_kernel, groups=groups, own=own),
        out_shape=(partial, partial),
        in_specs=[smem, smem, smem, vmem, hbm, vmem, vmem],
        out_specs=(vmem, vmem),
        scratch_shapes=[
            pltpu.VMEM((count, PIX, PIX), jnp.bfloat16),
            pltpu.VMEM((CLASSES * SLAB, PIX), jnp.float32),
            pltpu.SemaphoreType.DMA((count // CHUNK,)),
        ],
        compiler_params=pltpu.CompilerParams(vmem_limit_bytes=52 * MIB),
    )(
        me,
        class_ids,
        shifts.T,
        class_ids.reshape(count // PIX, PIX),
        images,
        jnp.asarray(column_table(pairs)),
        jnp.asarray(row_table()),
    )
    got = swap(send, "grp", 1)
    part = [(keep[q].astype(jnp.float32) + got[q].astype(jnp.float32)).astype(jnp.bfloat16) for q in range(nears)]
    met = [part[0]] + [hop(part[q], q, groups) for q in range(1, nears)]
    chip_sum = sum(m.astype(jnp.float32) for m in met).astype(jnp.bfloat16)
    pieces = [chip_sum[0]] + [swap(chip_sum[r], "dp", r << 1) for r in range(1, fars)]
    flat = BAND * BAND
    real, imag, rounded = pl.pallas_call(
        functools.partial(averages_kernel, own=own, parts=fars),
        out_shape=(
            jax.ShapeDtypeStruct((TILE, flat), jnp.float32),
            jax.ShapeDtypeStruct((TILE, flat), jnp.float32),
            jax.ShapeDtypeStruct((TILE, 2 * flat), jnp.bfloat16),
        ),
        in_specs=[vmem] * (fars + 2),
        out_specs=(vmem, vmem, vmem),
        scratch_shapes=[
            pltpu.VMEM((TILE * BAND, PIX), jnp.float32),
            pltpu.VMEM(((BAND + 1) * TILE, PIX), jnp.float32),
        ],
    )(*pieces, jnp.asarray(expand_table()), jnp.asarray(filter_table()))
    averages = jnp.stack([real[:own], imag[:own]], axis=1)
    held = [rounded] + [swap(rounded, "grp", k) for k in range(1, groups)]
    fresh = next_block.reshape(next_block.shape[0], 2 * flat)
    scores = pl.pallas_call(
        functools.partial(scores_kernel, own=own, groups=groups),
        out_shape=jax.ShapeDtypeStruct((own * groups, fresh.shape[0]), jnp.float32),
        in_specs=[smem] + [vmem] * (groups + 1),
        out_specs=vmem,
    )(me, *held, fresh)
    return averages, scores


def solution(mesh):
    placed = (
        P(("dp", "grp"), None, None),
        P(("dp", "grp"), None),
        P(("dp", "grp")),
        P("grp", None, None),
    )
    return jax.shard_map(
        body,
        mesh=mesh,
        in_specs=placed,
        out_specs=(P(("dp", "grp"), None, None), P("dp", "grp")),
        check_vma=False,
    )
```

```python
import functools
import math

import jax
import jax.numpy as jnp
import ml_dtypes
import numpy as np
from jax import lax
from jax.experimental import pallas as pl
from jax.experimental.pallas import tpu as pltpu
from jax.sharding import PartitionSpec as P

PIX = 128
BAND = 64
CLASSES = 256
HALF = BAND // 2
RIDGE = 4.0
REACH = 16
SLAB = PIX + 2 * REACH
TILE = 8
PACK = 16
ROWS = BAND + PACK
DIGITS = 4
CHUNK = 32
RING = 6
UNROLL = 32
MIB = 1 << 20


def basis():
    position = np.arange(PIX)
    freq = np.concatenate([np.arange(HALF + 1), np.arange(1, HALF + 1)])
    angle = (position[:, None] * freq[None, :] % PIX) * (2.0 * math.pi / PIX)
    is_cos = np.arange(BAND + 1) <= HALF
    table = np.where(is_cos[None, :], np.cos(angle), np.sin(angle)) / math.sqrt(PIX)
    return table.astype(np.float32).astype(ml_dtypes.bfloat16)


def column_table():
    table = basis()
    out = np.zeros((2 * PIX, PIX), ml_dtypes.bfloat16)
    for side in range(2):
        out[side * PIX : (side + 1) * PIX, side * BAND : (side + 1) * BAND] = table[:, :BAND]
    return out


def last_table(pairs):
    table = basis()
    out = np.zeros((pairs, PACK, 2 * PIX), ml_dtypes.bfloat16)
    for j in range(pairs):
        for side in range(2):
            out[j, j + side * pairs, side * PIX : (side + 1) * PIX] = table[:, BAND]
    return out


def row_table():
    out = np.zeros((ROWS, PIX), ml_dtypes.bfloat16)
    out[: BAND + 1] = basis().T
    return out


def expand_table():
    out = np.zeros((PIX, 2 * PIX), np.float32)
    for at in range(BAND):
        k = at - HALF
        for copy in range(2):
            out[abs(k), copy * BAND + at] = 1.0
            if k:
                row = BAND if abs(k) == HALF else HALF + abs(k)
                out[row, PIX + copy * BAND + at] = math.copysign(1.0, k)
    return out


def filter_table():
    squared = (np.arange(BAND, dtype=np.float32) - HALF) ** 2
    radius = squared[:, None] + squared[None, :]
    return np.exp(-radius / (BAND * BAND / 2.0)).reshape(BAND // 2, 2 * BAND).astype(np.float32)


def owner_of(near, far, other, groups):
    dp, grp = lax.axis_index("dp"), lax.axis_index("grp")
    there_dp = dp ^ ((far << 1) | (near & 1))
    there_grp = grp ^ (((near >> 1) << 1) | other)
    return there_dp * groups + there_grp


def sums_kernel(
    class_ids, pixel_shifts, images, acc, held, ids, shifts, sems, small_sem
):
    chunks = images.shape[0] // CHUNK

    def fetch(k):
        span = pl.ds(pl.multiple_of(k * CHUNK, CHUNK), CHUNK)
        slot = lax.rem(k, RING)
        return pltpu.make_async_copy(images.at[span], held.at[slot], sems.at[slot])

    small = [
        pltpu.make_async_copy(class_ids, ids, small_sem.at[0]),
        pltpu.make_async_copy(pixel_shifts, shifts, small_sem.at[1]),
    ]
    for copy in small:
        copy.start()
    for k in range(min(RING, chunks)):
        fetch(k).start()
    acc[...] = jnp.zeros_like(acc)
    for copy in small:
        copy.wait()

    def add_chunk(k, _):
        fetch(k).wait()
        slot = lax.rem(k, RING)

        def add_some(s, _):
            for u in range(UNROLL):
                i = k * CHUNK + s * UNROLL + u
                dx = shifts[0, i]
                at = ids[i] * SLAB + REACH + shifts[1, i]
                turned = pltpu.roll(
                    held[slot, s * UNROLL + u].astype(jnp.float32), jnp.where(dx < 0, dx + PIX, dx), 1
                )
                acc[pl.ds(at, PIX), :] = acc[pl.ds(at, PIX), :] + turned
            return 0

        lax.fori_loop(0, CHUNK // UNROLL, add_some, 0)

        @pl.when(k + RING < chunks)
        def _():
            fetch(k + RING).start()

        return 0

    lax.fori_loop(0, chunks, add_chunk, 0)


def transform_kernel(
    _, acc, ids_rows, col, row, last, block, out, fresh, edges, sems, *, near, other, groups, own
):
    pairs = own // 2
    fars = out.shape[0]
    together = 2 if fars % 2 == 0 else 1
    lane = lax.broadcasted_iota(jnp.int32, (TILE, ROWS), 1)
    sub = lax.broadcasted_iota(jnp.int32, (TILE, PIX), 0)
    edges[...] = jnp.zeros_like(edges)
    spans = fresh.shape[0]

    def regroup(f):
        at = ((2 * near + other) * spans + f) * PIX
        return pltpu.make_async_copy(block.at[:, :, pl.ds(at, PIX)], fresh.at[f], sems.at[f])

    for f in range(spans):
        regroup(f).start()

    def folded(c):
        at = pl.multiple_of(c * SLAB, TILE)
        head = acc[pl.ds(at + REACH, REACH), :] + acc[pl.ds(at + PIX + REACH, REACH), :]
        mid = acc[pl.ds(at + 2 * REACH, PIX - 2 * REACH), :]
        tail = acc[pl.ds(at + PIX, REACH), :] + acc[pl.ds(at, REACH), :]
        return jnp.concatenate([head, mid, tail], axis=0).astype(jnp.bfloat16)

    def transform(far, edge):
        owner = owner_of(near, far, other, groups)
        section = []
        ends = jnp.zeros((PACK, ROWS), jnp.float32)
        for j in range(pairs):
            both = jnp.concatenate(
                [folded(owner * own + j), folded(owner * own + j + pairs)], axis=1
            )
            part = jnp.dot(row[...], both, preferred_element_type=jnp.float32).astype(jnp.bfloat16)
            ends += lax.dot_general(
                last[j], part, (((1,), (1,)), ((), ())), preferred_element_type=jnp.float32
            )
            section.append(part)
        full = jnp.dot(
            jnp.concatenate(section, axis=0), col[...], preferred_element_type=jnp.float32
        )
        for j in range(pairs):
            at = j * ROWS
            out[far, j * BAND : (j + 1) * BAND, :] = full[at : at + BAND].astype(jnp.bfloat16)
            edge[j : j + 1, :] = full[at + BAND : at + BAND + 1]
        hits = jnp.zeros((TILE, PIX), jnp.float32)
        for r in range(ids_rows.shape[0]):
            hits += (ids_rows[r : r + 1, :] == owner * own + sub).astype(jnp.float32)
        rest = jnp.sum(hits, axis=1, keepdims=True)
        ends = ends[:TILE]
        for d in range(DIGITS):
            upper = jnp.floor(rest * 0.125) if d < DIGITS - 1 else jnp.zeros_like(rest)
            ends = jnp.where(lane == BAND + 1 + d, rest - 8.0 * upper, ends)
            rest = upper
        edge[TILE:, :ROWS] = ends
        out[far, pairs * BAND :, :] = edge[...].astype(jnp.bfloat16)

    def some(n, _):
        for k in range(together):
            transform(n * together + k, edges.at[k])
        return 0

    lax.fori_loop(0, fars // together, some, 0)
    for f in range(spans):
        regroup(f).wait()


def averages_kernel(*refs, own, parts):
    pieces, (expand, taper, real, imag, rounded, wide, rows) = refs[:parts], refs[parts:]
    pairs = own // 2
    total = pieces[0][...].astype(jnp.float32)
    for piece in pieces[1:]:
        total += piece[...].astype(jnp.float32)
    main, ends = total[: pairs * BAND], total[pairs * BAND :]
    if own < TILE:
        wide[...] = jnp.zeros_like(wide)
    wide[: pairs * BAND, :] = main
    wide[pairs * BAND : 2 * pairs * BAND, :] = pltpu.roll(main, BAND, 1)
    extra = ends[TILE:]
    lane = lax.broadcasted_iota(jnp.int32, (TILE, PIX), 1)
    for t in range(BAND + 1):
        if t < BAND:
            line = wide[pl.ds(t, TILE, stride=BAND), :]
        else:
            edge = ends[:pairs]
            line = jnp.concatenate([edge, pltpu.roll(ends[:TILE], BAND, 1)[:pairs]], axis=0)
            if own < TILE:
                line = jnp.concatenate([line, jnp.zeros((TILE - own, PIX), jnp.float32)], axis=0)
        line = jnp.where(
            lane < BAND, line, jnp.where(lane == BAND, extra[:, t : t + 1], 0.0)
        )
        rows[t * TILE : (t + 1) * TILE, :] = line
    spread = jnp.dot(
        rows[...], expand[...], preferred_element_type=jnp.float32, precision=lax.Precision.HIGHEST
    )

    def cos_part(t):
        return spread[t * TILE : (t + 1) * TILE, :PIX]

    def sin_part(t):
        return spread[t * TILE : (t + 1) * TILE, PIX:]

    members = jnp.zeros((TILE, 1), jnp.float32)
    for d in range(DIGITS):
        members += extra[:, BAND + 1 + d : BAND + 2 + d] * float(8**d)
    weight = members + RIDGE

    def at_frequency(k):
        c = abs(k)
        if k == 0:
            return cos_part(0), -sin_part(0)
        s = BAND if c == HALF else HALF + c
        if k > 0:
            return cos_part(c) - sin_part(s), -(cos_part(s) + sin_part(c))
        return cos_part(c) + sin_part(s), cos_part(s) - sin_part(c)

    for u in range(BAND // 2):
        even, odd = at_frequency(2 * u - HALF), at_frequency(2 * u + 1 - HALF)
        span = slice(u * PIX, (u + 1) * PIX)
        for part, out in ((0, real), (1, imag)):
            value = jnp.where(lane < BAND, even[part], odd[part]) * taper[u : u + 1, :] / weight
            out[:, span] = value
            at = part * BAND * BAND + u * PIX
            rounded[:, at : at + PIX] = value.astype(jnp.bfloat16)


def scores_kernel(*refs, own, groups):
    pieces, fresh, (out, sums) = refs[:groups], refs[groups:-2], refs[-2:]
    each = fresh[0].shape[0]
    spans = len(fresh) * each
    classes = own * groups
    held = jnp.concatenate([piece[:own] for piece in pieces], axis=0)
    both = jnp.concatenate([held[:, : spans * PIX], held[:, spans * PIX :]], axis=0)
    total = None
    for f in range(0, spans, 2):
        here = jnp.concatenate([fresh[g // each][g % each] for g in (f, f + 1)], axis=1)
        term = lax.dot_general(
            here,
            both[:, f * PIX : (f + 2) * PIX],
            (((1,), (1,)), ((), ())),
            preferred_element_type=jnp.float32,
        )
        total = term if total is None else total + term
    sums[:, : 2 * classes] = total
    count = out.shape[1]
    inner = sums[pl.ds(0, count, stride=2), :] + pltpu.roll(
        sums[pl.ds(1, count, stride=2), :], PIX - classes, 1
    )
    energy = jnp.sum(jnp.square(held.astype(jnp.float32)), axis=1, keepdims=True)
    result = (inner.T[:classes] - 0.5 * energy) / BAND
    for k in range(groups):
        at = (lax.axis_index("grp") ^ k) * own
        if own % TILE == 0:
            out[pl.ds(pl.multiple_of(at, TILE), own), :] = result[k * own : (k + 1) * own]
        else:
            for j in range(own):
                out[pl.ds(at + j, 1), :] = result[k * own + j : k * own + j + 1]


def swap(array, axis, flip):
    size = lax.axis_size(axis)
    return lax.ppermute(array, axis, [(i, i ^ flip) for i in range(size)])


def hop(array, near, groups):
    both = lax.axis_size("dp") * groups
    return lax.ppermute(
        array,
        ("dp", "grp"),
        [(i, i ^ ((near & 1) * groups | (near >> 1) * 2)) for i in range(both)],
    )


def body(images, shifts, class_ids, next_block):
    dp_count, groups = lax.axis_size("dp"), lax.axis_size("grp")
    own = CLASSES // (dp_count * groups)
    pairs = own // 2
    count = images.shape[0]
    nears, fars = groups, dp_count // 2
    block_rows = pairs * BAND + PACK
    vmem = pl.BlockSpec(memory_space=pltpu.VMEM)
    hbm = pl.BlockSpec(memory_space=pltpu.HBM)
    anywhere = pl.BlockSpec(memory_space=pl.ANY)
    flat = BAND * BAND
    spans = flat // PIX // (2 * nears)
    fresh_count = next_block.shape[0]

    def put(space, *arrays):
        return [pltpu.with_memory_space_constraint(a, space) for a in arrays]

    acc = pl.pallas_call(
        sums_kernel,
        out_shape=pltpu.VMEM((CLASSES * SLAB, PIX), jnp.float32),
        in_specs=[hbm] * 3,
        out_specs=vmem,
        scratch_shapes=[
            pltpu.VMEM((RING, CHUNK, PIX, PIX), jnp.bfloat16),
            pltpu.SMEM((count,), jnp.int32),
            pltpu.SMEM((2, count), jnp.int32),
            pltpu.SemaphoreType.DMA((RING,)),
            pltpu.SemaphoreType.DMA((2,)),
        ],
        compiler_params=pltpu.CompilerParams(vmem_limit_bytes=10 * MIB),
    )(*put(pltpu.HBM, class_ids, shifts.T, images))
    piece = jax.ShapeDtypeStruct((fars, block_rows, PIX), jnp.bfloat16)
    ids_rows = class_ids.reshape(count // PIX, PIX)
    tables = [jnp.asarray(t) for t in (column_table(), row_table(), last_table(pairs))]

    (block,) = put(pltpu.HBM, next_block)
    (held_acc,) = put(pltpu.VMEM, acc)

    def transform(after, near, other):
        return pl.pallas_call(
            functools.partial(transform_kernel, near=near, other=other, groups=groups, own=own),
            out_shape=(piece, pltpu.VMEM((spans, fresh_count, 2, PIX), jnp.bfloat16)),
            in_specs=[anywhere] + [vmem] * 5 + [hbm],
            out_specs=(vmem, vmem),
            scratch_shapes=[
                pltpu.VMEM((2, PACK, PIX), jnp.float32),
                pltpu.SemaphoreType.DMA((spans,)),
            ],
            compiler_params=pltpu.CompilerParams(vmem_limit_bytes=8 * MIB),
            cost_estimate=pl.CostEstimate(flops=10**10, bytes_accessed=MIB, transcendentals=0),
        )(after, held_acc, ids_rows, *tables, block)

    met = [None] * nears
    done = ids_rows
    fresh = [None] * (2 * nears)
    for near in reversed(range(nears)):
        send, fresh[2 * near + 1] = transform(done, near, 1)
        got = swap(send, "grp", 1)
        keep, fresh[2 * near] = transform(send, near, 0)
        part = (keep.astype(jnp.float32) + got.astype(jnp.float32)).astype(jnp.bfloat16)
        met[near] = hop(part, near, groups) if near else part
        done = part
    chip_sum = sum(m.astype(jnp.float32) for m in met).astype(jnp.bfloat16)
    pieces = [chip_sum[0]] + [swap(chip_sum[r], "dp", r << 1) for r in range(1, fars)]
    real, imag, rounded = pl.pallas_call(
        functools.partial(averages_kernel, own=own, parts=fars),
        out_shape=(
            jax.ShapeDtypeStruct((TILE, flat), jnp.float32),
            jax.ShapeDtypeStruct((TILE, flat), jnp.float32),
            jax.ShapeDtypeStruct((TILE, 2 * flat), jnp.bfloat16),
        ),
        in_specs=[vmem] * (fars + 2),
        out_specs=(vmem, vmem, vmem),
        scratch_shapes=[
            pltpu.VMEM((TILE * BAND, PIX), jnp.float32),
            pltpu.VMEM(((BAND + 1) * TILE, PIX), jnp.float32),
        ],
        compiler_params=pltpu.CompilerParams(vmem_limit_bytes=8 * MIB),
    )(*put(pltpu.VMEM, *pieces), jnp.asarray(expand_table()), jnp.asarray(filter_table()))
    averages = jnp.stack([real[:own], imag[:own]], axis=1)
    held = [rounded] + [swap(rounded, "grp", k) for k in range(1, groups)]
    fresh = [f.reshape(spans, 2 * fresh_count, PIX) for f in fresh]
    scores = pl.pallas_call(
        functools.partial(scores_kernel, own=own, groups=groups),
        out_shape=jax.ShapeDtypeStruct((own * groups, fresh_count), jnp.float32),
        in_specs=[vmem] * (groups + len(fresh)),
        out_specs=vmem,
        scratch_shapes=[pltpu.VMEM((2 * fresh_count, PIX), jnp.float32)],
        compiler_params=pltpu.CompilerParams(vmem_limit_bytes=16 * MIB),
    )(*put(pltpu.VMEM, *held, *fresh))
    return averages, scores


def solution(mesh):
    placed = (
        P(("dp", "grp"), None, None),
        P(("dp", "grp"), None),
        P(("dp", "grp")),
        P("grp", None, None),
    )
    return jax.shard_map(
        body,
        mesh=mesh,
        in_specs=placed,
        out_specs=(P(("dp", "grp"), None, None), P("dp", "grp")),
        check_vma=False,
    )
```

```python
import functools
import math

import jax
import jax.numpy as jnp
import ml_dtypes
import numpy as np
from jax import lax
from jax.experimental import pallas as pl
from jax.experimental.pallas import tpu as pltpu
from jax.sharding import PartitionSpec as P

PIX = 128
BAND = 64
CLASSES = 256
HALF = BAND // 2
RIDGE = 4.0
REACH = 16
SLAB = PIX + 2 * REACH
TILE = 8
PACK = 16
ROWS = BAND + PACK
DIGITS = 4
CHUNK = 32
RING = 6
UNROLL = 32
MIB = 1 << 20


def basis():
    position = np.arange(PIX)
    freq = np.concatenate([np.arange(HALF + 1), np.arange(1, HALF + 1)])
    angle = (position[:, None] * freq[None, :] % PIX) * (2.0 * math.pi / PIX)
    is_cos = np.arange(BAND + 1) <= HALF
    table = np.where(is_cos[None, :], np.cos(angle), np.sin(angle)) / math.sqrt(PIX)
    return table.astype(np.float32).astype(ml_dtypes.bfloat16)


def column_table():
    table = basis()
    out = np.zeros((2 * PIX, PIX), ml_dtypes.bfloat16)
    for side in range(2):
        out[side * PIX : (side + 1) * PIX, side * BAND : (side + 1) * BAND] = table[:, :BAND]
    return out


def last_table(pairs):
    table = basis()
    out = np.zeros((PACK, pairs, 2 * PIX), ml_dtypes.bfloat16)
    for j in range(pairs):
        for side in range(2):
            out[j + side * pairs, j, side * PIX : (side + 1) * PIX] = table[:, BAND]
    return out.reshape(PACK, -1)


def row_table():
    out = np.zeros((ROWS, PIX), ml_dtypes.bfloat16)
    out[: BAND + 1] = basis().T
    return out


def expand_table():
    out = np.zeros((PIX, 2 * PIX), np.float32)
    for at in range(BAND):
        k = at - HALF
        for copy in range(2):
            out[abs(k), copy * BAND + at] = 1.0
            if k:
                row = BAND if abs(k) == HALF else HALF + abs(k)
                out[row, PIX + copy * BAND + at] = math.copysign(1.0, k)
    return out


def filter_table():
    squared = (np.arange(BAND, dtype=np.float32) - HALF) ** 2
    radius = squared[:, None] + squared[None, :]
    return np.exp(-radius / (BAND * BAND / 2.0)).reshape(BAND // 2, 2 * BAND).astype(np.float32)


def owner_of(near, far, other, groups):
    dp, grp = lax.axis_index("dp"), lax.axis_index("grp")
    there_dp = dp ^ ((far << 1) | (near & 1))
    there_grp = grp ^ (((near >> 1) << 1) | other)
    return there_dp * groups + there_grp


def sums_kernel(
    class_ids, pixel_shifts, images, acc, held, ids, shifts, sems, small_sem
):
    chunks = images.shape[0] // CHUNK

    def fetch(k):
        span = pl.ds(pl.multiple_of(k * CHUNK, CHUNK), CHUNK)
        slot = lax.rem(k, RING)
        return pltpu.make_async_copy(images.at[span], held.at[slot], sems.at[slot])

    small = [
        pltpu.make_async_copy(class_ids, ids, small_sem.at[0]),
        pltpu.make_async_copy(pixel_shifts, shifts, small_sem.at[1]),
    ]
    for copy in small:
        copy.start()
    for k in range(min(RING, chunks)):
        fetch(k).start()
    acc[...] = jnp.zeros_like(acc)
    for copy in small:
        copy.wait()

    def add_chunk(k, _):
        fetch(k).wait()
        slot = lax.rem(k, RING)

        def add_some(s, _):
            for u in range(UNROLL):
                i = k * CHUNK + s * UNROLL + u
                dx = shifts[0, i]
                at = ids[i] * SLAB + REACH + shifts[1, i]
                turned = pltpu.roll(
                    held[slot, s * UNROLL + u].astype(jnp.float32), jnp.where(dx < 0, dx + PIX, dx), 1
                )
                acc[pl.ds(at, PIX), :] = acc[pl.ds(at, PIX), :] + turned
            return 0

        lax.fori_loop(0, CHUNK // UNROLL, add_some, 0)

        @pl.when(k + RING < chunks)
        def _():
            fetch(k + RING).start()

        return 0

    lax.fori_loop(0, chunks, add_chunk, 0)


def transform_kernel(
    _, acc, ids_rows, col, row, last, block, out, fresh, edges, sems, *, jobs, step, other, groups, own
):
    pairs = own // 2
    count = out.shape[0]
    half = count // len(jobs)
    together = 2 if count % 2 == 0 else 1
    lane = lax.broadcasted_iota(jnp.int32, (TILE, ROWS), 1)
    sub = lax.broadcasted_iota(jnp.int32, (TILE, PIX), 0)
    edges[...] = jnp.zeros_like(edges)
    spans = fresh.shape[0]

    def regroup(f):
        at = (step * spans + f) * PIX
        return pltpu.make_async_copy(block.at[:, :, pl.ds(at, PIX)], fresh.at[f], sems.at[f])

    for f in range(spans):
        regroup(f).start()

    def folded(c):
        at = pl.multiple_of(c * SLAB, TILE)
        head = acc[pl.ds(at + REACH, REACH), :] + acc[pl.ds(at + PIX + REACH, REACH), :]
        mid = acc[pl.ds(at + 2 * REACH, PIX - 2 * REACH), :]
        tail = acc[pl.ds(at + PIX, REACH), :] + acc[pl.ds(at, REACH), :]
        return jnp.concatenate([head, mid, tail], axis=0).astype(jnp.bfloat16)

    def transform(far, edge):
        near, first = jobs[-1]
        which = lax.div(far, half)
        for k, job in enumerate(jobs[:-1]):
            near = jnp.where(which == k, job[0], near)
            first = jnp.where(which == k, job[1], first)
        owner = owner_of(near, first + lax.rem(far, half), other, groups)
        wide = jnp.concatenate(
            [folded(owner * own + j + side * pairs) for j in range(pairs) for side in range(2)], axis=1
        )
        part = jnp.dot(row[...], wide, preferred_element_type=jnp.float32).astype(jnp.bfloat16)
        ends = lax.dot_general(
            last[...], part, (((1,), (1,)), ((), ())), preferred_element_type=jnp.float32
        )
        full = jnp.dot(
            jnp.concatenate(
                [part[:, 2 * PIX * j : 2 * PIX * (j + 1)] for j in range(pairs)], axis=0
            ),
            col[...],
            preferred_element_type=jnp.float32,
        )
        for j in range(pairs):
            at = j * ROWS
            out[far, j * BAND : (j + 1) * BAND, :] = full[at : at + BAND].astype(jnp.bfloat16)
            edge[j : j + 1, :] = full[at + BAND : at + BAND + 1]
        hits = jnp.zeros((TILE, PIX), jnp.float32)
        for r in range(ids_rows.shape[0]):
            hits += (ids_rows[r : r + 1, :] == owner * own + sub).astype(jnp.float32)
        rest = jnp.sum(hits, axis=1, keepdims=True)
        ends = ends[:TILE]
        for d in range(DIGITS):
            upper = jnp.floor(rest * 0.125) if d < DIGITS - 1 else jnp.zeros_like(rest)
            ends = jnp.where(lane == BAND + 1 + d, rest - 8.0 * upper, ends)
            rest = upper
        edge[TILE:, :ROWS] = ends
        out[far, pairs * BAND :, :] = edge[...].astype(jnp.bfloat16)

    def some(n, _):
        for k in range(together):
            transform(n * together + k, edges.at[k])
        return 0

    lax.fori_loop(0, count // together, some, 0)
    for f in range(spans):
        regroup(f).wait()


def totals_kernel(_, *refs, parts):
    for r, out in enumerate(refs[parts:]):
        total = refs[0][r].astype(jnp.float32)
        for ref in refs[1:parts]:
            total += ref[r].astype(jnp.float32)
        out[...] = total.astype(jnp.bfloat16)


def averages_kernel(*refs, own, parts):
    pieces, (expand, taper, real, imag, rounded, wide, rows) = refs[:parts], refs[parts:]
    pairs = own // 2
    total = pieces[0][...].astype(jnp.float32)
    for piece in pieces[1:]:
        total += piece[...].astype(jnp.float32)
    main, ends = total[: pairs * BAND], total[pairs * BAND :]
    if own < TILE:
        wide[...] = jnp.zeros_like(wide)
    wide[: pairs * BAND, :] = main
    wide[pairs * BAND : 2 * pairs * BAND, :] = pltpu.roll(main, BAND, 1)
    extra = ends[TILE:]
    lane = lax.broadcasted_iota(jnp.int32, (TILE, PIX), 1)
    for t in range(BAND + 1):
        if t < BAND:
            line = wide[pl.ds(t, TILE, stride=BAND), :]
        else:
            edge = ends[:pairs]
            line = jnp.concatenate([edge, pltpu.roll(ends[:TILE], BAND, 1)[:pairs]], axis=0)
            if own < TILE:
                line = jnp.concatenate([line, jnp.zeros((TILE - own, PIX), jnp.float32)], axis=0)
        line = jnp.where(
            lane < BAND, line, jnp.where(lane == BAND, extra[:, t : t + 1], 0.0)
        )
        rows[t * TILE : (t + 1) * TILE, :] = line
    spread = jnp.dot(
        rows[...], expand[...], preferred_element_type=jnp.float32, precision=lax.Precision.HIGHEST
    )

    def cos_part(t):
        return spread[t * TILE : (t + 1) * TILE, :PIX]

    def sin_part(t):
        return spread[t * TILE : (t + 1) * TILE, PIX:]

    members = jnp.zeros((TILE, 1), jnp.float32)
    for d in range(DIGITS):
        members += extra[:, BAND + 1 + d : BAND + 2 + d] * float(8**d)
    weight = members + RIDGE

    def at_frequency(k):
        c = abs(k)
        if k == 0:
            return cos_part(0), -sin_part(0)
        s = BAND if c == HALF else HALF + c
        if k > 0:
            return cos_part(c) - sin_part(s), -(cos_part(s) + sin_part(c))
        return cos_part(c) + sin_part(s), cos_part(s) - sin_part(c)

    for u in range(BAND // 2):
        even, odd = at_frequency(2 * u - HALF), at_frequency(2 * u + 1 - HALF)
        span = slice(u * PIX, (u + 1) * PIX)
        for part, out in ((0, real), (1, imag)):
            value = jnp.where(lane < BAND, even[part], odd[part]) * taper[u : u + 1, :] / weight
            out[:, span] = value
            at = part * BAND * BAND + u * PIX
            rounded[:, at : at + PIX] = value.astype(jnp.bfloat16)


def scores_kernel(*refs, own, groups):
    pieces, fresh, (out, sums) = refs[:groups], refs[groups:-2], refs[-2:]
    each = fresh[0].shape[0]
    spans = len(fresh) * each
    classes = own * groups
    held = jnp.concatenate([piece[:own] for piece in pieces], axis=0)
    both = jnp.concatenate([held[:, : spans * PIX], held[:, spans * PIX :]], axis=0)
    total = None
    for f in range(0, spans, 2):
        here = jnp.concatenate([fresh[g // each][g % each] for g in (f, f + 1)], axis=1)
        term = lax.dot_general(
            here,
            both[:, f * PIX : (f + 2) * PIX],
            (((1,), (1,)), ((), ())),
            preferred_element_type=jnp.float32,
        )
        total = term if total is None else total + term
    sums[:, : 2 * classes] = total
    count = out.shape[1]
    inner = sums[pl.ds(0, count, stride=2), :] + pltpu.roll(
        sums[pl.ds(1, count, stride=2), :], PIX - classes, 1
    )
    energy = jnp.sum(jnp.square(held.astype(jnp.float32)), axis=1, keepdims=True)
    result = (inner.T[:classes] - 0.5 * energy) / BAND
    for k in range(groups):
        at = (lax.axis_index("grp") ^ k) * own
        if own % TILE == 0:
            out[pl.ds(pl.multiple_of(at, TILE), own), :] = result[k * own : (k + 1) * own]
        else:
            for j in range(own):
                out[pl.ds(at + j, 1), :] = result[k * own + j : k * own + j + 1]


def swap(array, axis, flip):
    size = lax.axis_size(axis)
    return lax.ppermute(array, axis, [(i, i ^ flip) for i in range(size)])


def hop(array, near, groups):
    both = lax.axis_size("dp") * groups
    return lax.ppermute(
        array,
        ("dp", "grp"),
        [(i, i ^ ((near & 1) * groups | (near >> 1) * 2)) for i in range(both)],
    )


def body(images, shifts, class_ids, next_block):
    dp_count, groups = lax.axis_size("dp"), lax.axis_size("grp")
    own = CLASSES // (dp_count * groups)
    pairs = own // 2
    count = images.shape[0]
    nears, fars = groups, dp_count // 2
    block_rows = pairs * BAND + PACK
    vmem = pl.BlockSpec(memory_space=pltpu.VMEM)
    hbm = pl.BlockSpec(memory_space=pltpu.HBM)
    anywhere = pl.BlockSpec(memory_space=pl.ANY)
    flat = BAND * BAND
    spans = flat // PIX // (2 * nears)
    fresh_count = next_block.shape[0]

    def put(space, *arrays):
        return [pltpu.with_memory_space_constraint(a, space) for a in arrays]

    acc = pl.pallas_call(
        sums_kernel,
        out_shape=pltpu.VMEM((CLASSES * SLAB, PIX), jnp.float32),
        in_specs=[hbm] * 3,
        out_specs=vmem,
        scratch_shapes=[
            pltpu.VMEM((RING, CHUNK, PIX, PIX), jnp.bfloat16),
            pltpu.SMEM((count,), jnp.int32),
            pltpu.SMEM((2, count), jnp.int32),
            pltpu.SemaphoreType.DMA((RING,)),
            pltpu.SemaphoreType.DMA((2,)),
        ],
        compiler_params=pltpu.CompilerParams(vmem_limit_bytes=10 * MIB),
    )(*put(pltpu.HBM, class_ids, shifts.T, images))
    half = fars // 2
    piece = jax.ShapeDtypeStruct((2 * half, block_rows, PIX), jnp.bfloat16)
    ids_rows = class_ids.reshape(count // PIX, PIX)
    tables = [jnp.asarray(t) for t in (column_table(), row_table(), last_table(pairs))]

    (block,) = put(pltpu.HBM, next_block)
    (held_acc,) = put(pltpu.VMEM, acc)

    fresh = []

    def transform(after, jobs, other):
        out, block_part = pl.pallas_call(
            functools.partial(
                transform_kernel, jobs=jobs, step=len(fresh), other=other, groups=groups, own=own
            ),
            out_shape=(piece, pltpu.VMEM((spans, fresh_count, 2, PIX), jnp.bfloat16)),
            in_specs=[anywhere] + [vmem] * 5 + [hbm],
            out_specs=(vmem, vmem),
            scratch_shapes=[
                pltpu.VMEM((2, PACK, PIX), jnp.float32),
                pltpu.SemaphoreType.DMA((spans,)),
            ],
            compiler_params=pltpu.CompilerParams(vmem_limit_bytes=8 * MIB),
            cost_estimate=pl.CostEstimate(flops=10**10, bytes_accessed=MIB, transcendentals=0),
        )(after, held_acc, ids_rows, *tables, block)
        fresh.append(block_part)
        return out

    met = {half: [], 0: []}
    done = ids_rows
    for first in (half, 0):
        for nears_here in ((3, 2), (1, 0)):
            jobs = tuple((near, first) for near in nears_here)
            send = transform(done, jobs, 1)
            got = swap(send, "grp", 1)
            keep = transform(send, jobs, 0)
            for k, near in enumerate(nears_here):
                span = slice(k * half, (k + 1) * half)
                part = keep[span].astype(jnp.float32) + got[span].astype(jnp.float32)
                part = part.astype(jnp.bfloat16)
                met[first].append(hop(part, near, groups) if near else part)
            done = part
    pieces = [None] * fars
    for first in (half, 0):
        totals = pl.pallas_call(
            functools.partial(totals_kernel, parts=nears),
            out_shape=[jax.ShapeDtypeStruct((block_rows, PIX), jnp.bfloat16)] * half,
            in_specs=[anywhere] + [vmem] * nears,
            out_specs=[vmem] * half,
            compiler_params=pltpu.CompilerParams(vmem_limit_bytes=8 * MIB),
        )(done, *met[first])
        for r, total in enumerate(totals):
            far = first + r
            pieces[far] = swap(total, "dp", far << 1) if far else total
        done = totals[0]
    real, imag, rounded = pl.pallas_call(
        functools.partial(averages_kernel, own=own, parts=fars),
        out_shape=(
            jax.ShapeDtypeStruct((TILE, flat), jnp.float32),
            jax.ShapeDtypeStruct((TILE, flat), jnp.float32),
            jax.ShapeDtypeStruct((TILE, 2 * flat), jnp.bfloat16),
        ),
        in_specs=[vmem] * (fars + 2),
        out_specs=(vmem, vmem, vmem),
        scratch_shapes=[
            pltpu.VMEM((TILE * BAND, PIX), jnp.float32),
            pltpu.VMEM(((BAND + 1) * TILE, PIX), jnp.float32),
        ],
        compiler_params=pltpu.CompilerParams(vmem_limit_bytes=8 * MIB),
    )(*put(pltpu.VMEM, *pieces), jnp.asarray(expand_table()), jnp.asarray(filter_table()))
    averages = jnp.stack([real[:own], imag[:own]], axis=1)
    held = [rounded, swap(rounded, "grp", 1)]
    for k in range(2, groups, 2):
        across = swap(rounded, "grp", k)
        held += [across, swap(across, "grp", 1)]
    fresh = [f.reshape(spans, 2 * fresh_count, PIX) for f in fresh]
    scores = pl.pallas_call(
        functools.partial(scores_kernel, own=own, groups=groups),
        out_shape=jax.ShapeDtypeStruct((own * groups, fresh_count), jnp.float32),
        in_specs=[vmem] * (groups + len(fresh)),
        out_specs=vmem,
        scratch_shapes=[pltpu.VMEM((2 * fresh_count, PIX), jnp.float32)],
        compiler_params=pltpu.CompilerParams(vmem_limit_bytes=16 * MIB),
    )(*put(pltpu.VMEM, *held, *fresh))
    return averages, scores


def solution(mesh):
    placed = (
        P(("dp", "grp"), None, None),
        P(("dp", "grp"), None),
        P(("dp", "grp")),
        P("grp", None, None),
    )
    return jax.shard_map(
        body,
        mesh=mesh,
        in_specs=placed,
        out_specs=(P(("dp", "grp"), None, None), P("dp", "grp")),
        check_vma=False,
    )
```

```python
import functools
import math

import jax
import jax.numpy as jnp
import ml_dtypes
import numpy as np
from jax import lax
from jax.experimental import pallas as pl
from jax.experimental.pallas import tpu as pltpu
from jax.sharding import PartitionSpec as P

PIX = 128
BAND = 64
CLASSES = 256
HALF = BAND // 2
RIDGE = 4.0
REACH = 16
SLAB = PIX + 2 * REACH
TILE = 8
PACK = 16
ROWS = BAND + PACK
DIGITS = 4
CHUNK = 32
RING = 6
UNROLL = 32
MIB = 1 << 20


def basis():
    position = np.arange(PIX)
    freq = np.concatenate([np.arange(HALF + 1), np.arange(1, HALF + 1)])
    angle = (position[:, None] * freq[None, :] % PIX) * (2.0 * math.pi / PIX)
    is_cos = np.arange(BAND + 1) <= HALF
    table = np.where(is_cos[None, :], np.cos(angle), np.sin(angle)) / math.sqrt(PIX)
    return table.astype(np.float32).astype(ml_dtypes.bfloat16)


def column_table():
    table = basis()
    out = np.zeros((2 * PIX, PIX), ml_dtypes.bfloat16)
    for side in range(2):
        out[side * PIX : (side + 1) * PIX, side * BAND : (side + 1) * BAND] = table[:, :BAND]
    return out


def last_table(pairs):
    table = basis()
    out = np.zeros((PACK, pairs, 2 * PIX), ml_dtypes.bfloat16)
    for j in range(pairs):
        for side in range(2):
            out[j + side * pairs, j, side * PIX : (side + 1) * PIX] = table[:, BAND]
    return out.reshape(PACK, -1)


def row_table():
    out = np.zeros((ROWS, PIX), ml_dtypes.bfloat16)
    out[: BAND + 1] = basis().T
    return out


def expand_table():
    out = np.zeros((PIX, 2 * PIX), ml_dtypes.bfloat16)
    for at in range(BAND):
        k = at - HALF
        for copy in range(2):
            out[abs(k), copy * BAND + at] = 1.0
            if k:
                row = BAND if abs(k) == HALF else HALF + abs(k)
                out[row, PIX + copy * BAND + at] = math.copysign(1.0, k)
    return out


def filter_table():
    squared = (np.arange(BAND, dtype=np.float32) - HALF) ** 2
    radius = squared[:, None] + squared[None, :]
    return np.exp(-radius / (BAND * BAND / 2.0)).reshape(BAND // 2, 2 * BAND).astype(np.float32)


def owner_of(near, far, other, groups):
    dp, grp = lax.axis_index("dp"), lax.axis_index("grp")
    there_dp = dp ^ ((far << 1) | (near & 1))
    there_grp = grp ^ (((near >> 1) << 1) | other)
    return there_dp * groups + there_grp


def sums_kernel(
    class_ids, pixel_shifts, images, acc, held, ids, shifts, sems, small_sem
):
    chunks = images.shape[0] // CHUNK

    def fetch(k):
        span = pl.ds(pl.multiple_of(k * CHUNK, CHUNK), CHUNK)
        slot = lax.rem(k, RING)
        return pltpu.make_async_copy(images.at[span], held.at[slot], sems.at[slot])

    small = [
        pltpu.make_async_copy(class_ids, ids, small_sem.at[0]),
        pltpu.make_async_copy(pixel_shifts, shifts, small_sem.at[1]),
    ]
    for copy in small:
        copy.start()
    for k in range(min(RING, chunks)):
        fetch(k).start()
    acc[...] = jnp.zeros_like(acc)
    for copy in small:
        copy.wait()

    def add_chunk(k, _):
        fetch(k).wait()
        slot = lax.rem(k, RING)

        def add_some(s, _):
            for u in range(UNROLL):
                i = k * CHUNK + s * UNROLL + u
                dx = shifts[0, i]
                at = ids[i] * SLAB + REACH + shifts[1, i]
                turned = pltpu.roll(
                    held[slot, s * UNROLL + u].astype(jnp.float32), jnp.where(dx < 0, dx + PIX, dx), 1
                )
                acc[pl.ds(at, PIX), :] = acc[pl.ds(at, PIX), :] + turned
            return 0

        lax.fori_loop(0, CHUNK // UNROLL, add_some, 0)

        @pl.when(k + RING < chunks)
        def _():
            fetch(k + RING).start()

        return 0

    lax.fori_loop(0, chunks, add_chunk, 0)


def transform_kernel(
    _, acc, ids_rows, col, row, last, out, edges, *, jobs, other, groups, own
):
    pairs = own // 2
    count = out.shape[0]
    half = count // len(jobs)
    together = 4 if count % 4 == 0 else 1
    lane = lax.broadcasted_iota(jnp.int32, (TILE, ROWS), 1)
    sub = lax.broadcasted_iota(jnp.int32, (TILE, PIX), 0)
    edges[...] = jnp.zeros_like(edges)

    def folded(c):
        at = pl.multiple_of(c * SLAB, TILE)
        head = acc[pl.ds(at + REACH, REACH), :] + acc[pl.ds(at + PIX + REACH, REACH), :]
        mid = acc[pl.ds(at + 2 * REACH, PIX - 2 * REACH), :]
        tail = acc[pl.ds(at + PIX, REACH), :] + acc[pl.ds(at, REACH), :]
        return jnp.concatenate([head, mid, tail], axis=0).astype(jnp.bfloat16)

    def transform(far, edge):
        near, first = jobs[-1]
        which = lax.div(far, half)
        for k, job in enumerate(jobs[:-1]):
            near = jnp.where(which == k, job[0], near)
            first = jnp.where(which == k, job[1], first)
        owner = owner_of(near, first + lax.rem(far, half), other, groups)
        wide = jnp.concatenate(
            [folded(owner * own + j + side * pairs) for j in range(pairs) for side in range(2)], axis=1
        )
        part = jnp.dot(row[...], wide, preferred_element_type=jnp.float32).astype(jnp.bfloat16)
        ends = lax.dot_general(
            last[...], part, (((1,), (1,)), ((), ())), preferred_element_type=jnp.float32
        )
        full = jnp.dot(
            jnp.concatenate(
                [part[:, 2 * PIX * j : 2 * PIX * (j + 1)] for j in range(pairs)], axis=0
            ),
            col[...],
            preferred_element_type=jnp.float32,
        )
        for j in range(pairs):
            at = j * ROWS
            out[far, j * BAND : (j + 1) * BAND, :] = full[at : at + BAND].astype(jnp.bfloat16)
            edge[j : j + 1, :] = full[at + BAND : at + BAND + 1]
        hits = jnp.zeros((TILE, PIX), jnp.float32)
        for r in range(ids_rows.shape[0]):
            hits += (ids_rows[r : r + 1, :] == owner * own + sub).astype(jnp.float32)
        rest = jnp.sum(hits, axis=1, keepdims=True)
        ends = ends[:TILE]
        for d in range(DIGITS):
            upper = jnp.floor(rest * 0.125) if d < DIGITS - 1 else jnp.zeros_like(rest)
            ends = jnp.where(lane == BAND + 1 + d, rest - 8.0 * upper, ends)
            rest = upper
        edge[TILE:, :ROWS] = ends
        out[far, pairs * BAND :, :] = edge[...].astype(jnp.bfloat16)

    def some(n, _):
        for k in range(together):
            transform(n * together + k, edges.at[k])
        return 0

    lax.fori_loop(0, count // together, some, 0)


def regroup_kernel(_, block, fresh, sems):
    copies = [
        pltpu.make_async_copy(block.at[:, :, pl.ds(f * PIX, PIX)], fresh.at[f], sems.at[f])
        for f in range(fresh.shape[0])
    ]
    for copy in copies:
        copy.start()
    for copy in copies:
        copy.wait()


def totals_kernel(_, *refs, parts):
    for r, out in enumerate(refs[parts:]):
        total = refs[0][r].astype(jnp.float32)
        for ref in refs[1:parts]:
            total += ref[r].astype(jnp.float32)
        out[...] = total.astype(jnp.bfloat16)


def added(pieces):
    total = pieces[0][...].astype(jnp.float32)
    for piece in pieces[1:]:
        total += piece[...].astype(jnp.float32)
    return total


def added_kernel(*refs):
    refs[-1][...] = added(refs[:-1]).astype(jnp.bfloat16)


def averages_kernel(*refs, own, parts):
    pieces, (expand, taper, out, rounded, wide, rows) = refs[:parts], refs[parts:]

    def emit(u, part, value):
        out[:, part, u * PIX : (u + 1) * PIX] = value[:own]
        at = part * BAND * BAND + u * PIX
        rounded[:, at : at + PIX] = value.astype(jnp.bfloat16)

    spread_out(added(pieces), 3, expand, taper, wide, rows, own, emit)


def references_kernel(*refs, own):
    _, piece, expand, taper, rounded, wide, rows = refs

    def emit(u, part, value):
        at = part * BAND * BAND + u * PIX
        rounded[:, at : at + PIX] = value.astype(jnp.bfloat16)

    spread_out(piece[...].astype(jnp.float32), 1, expand, taper, wide, rows, own, emit)


def spread_out(total, pieces, expand, taper, wide, rows, own, emit):
    pairs = own // 2
    main, ends = total[: pairs * BAND], total[pairs * BAND :]
    if own < TILE:
        wide[...] = jnp.zeros_like(wide)
    wide[: pairs * BAND, :] = main
    wide[pairs * BAND : 2 * pairs * BAND, :] = pltpu.roll(main, BAND, 1)
    extra = ends[TILE:]
    lane = lax.broadcasted_iota(jnp.int32, (TILE, PIX), 1)
    for t in range(BAND + 1):
        if t < BAND:
            line = wide[pl.ds(t, TILE, stride=BAND), :]
        else:
            edge = ends[:pairs]
            line = jnp.concatenate([edge, pltpu.roll(ends[:TILE], BAND, 1)[:pairs]], axis=0)
            if own < TILE:
                line = jnp.concatenate([line, jnp.zeros((TILE - own, PIX), jnp.float32)], axis=0)
        line = jnp.where(
            lane < BAND, line, jnp.where(lane == BAND, extra[:, t : t + 1], 0.0)
        )
        rows[t * TILE : (t + 1) * TILE, :] = line
    spread = None
    rest = rows[...]
    for k in range(pieces):
        here = rest.astype(jnp.bfloat16)
        rest = rest - here.astype(jnp.float32) if k + 1 < pieces else None
        term = jnp.dot(here, expand[...], preferred_element_type=jnp.float32)
        spread = term if spread is None else spread + term

    def cos_part(t):
        return spread[t * TILE : (t + 1) * TILE, :PIX]

    def sin_part(t):
        return spread[t * TILE : (t + 1) * TILE, PIX:]

    members = jnp.zeros((TILE, 1), jnp.float32)
    for d in range(DIGITS):
        members += extra[:, BAND + 1 + d : BAND + 2 + d] * float(8**d)
    weight = members + RIDGE

    def at_frequency(k):
        c = abs(k)
        if k == 0:
            return cos_part(0), -sin_part(0)
        s = BAND if c == HALF else HALF + c
        if k > 0:
            return cos_part(c) - sin_part(s), -(cos_part(s) + sin_part(c))
        return cos_part(c) + sin_part(s), cos_part(s) - sin_part(c)

    for u in range(BAND // 2):
        even, odd = at_frequency(2 * u - HALF), at_frequency(2 * u + 1 - HALF)
        for part in range(2):
            value = jnp.where(lane < BAND, even[part], odd[part]) * taper[u : u + 1, :] / weight
            emit(u, part, value)


def scores_kernel(*refs, own, groups):
    pieces, fresh, (out, sums) = refs[:groups], refs[groups:-2], refs[-2:]
    each = fresh[0].shape[0]
    spans = len(fresh) * each
    classes = own * groups
    held = jnp.concatenate([piece[:own] for piece in pieces], axis=0)
    both = jnp.concatenate([held[:, : spans * PIX], held[:, spans * PIX :]], axis=0)
    total = None
    for f in range(0, spans, 2):
        here = jnp.concatenate([fresh[g // each][g % each] for g in (f, f + 1)], axis=1)
        term = lax.dot_general(
            here,
            both[:, f * PIX : (f + 2) * PIX],
            (((1,), (1,)), ((), ())),
            preferred_element_type=jnp.float32,
        )
        total = term if total is None else total + term
    sums[:, : 2 * classes] = total
    count = out.shape[1]
    inner = sums[pl.ds(0, count, stride=2), :] + pltpu.roll(
        sums[pl.ds(1, count, stride=2), :], PIX - classes, 1
    )
    energy = jnp.sum(jnp.square(held.astype(jnp.float32)), axis=1, keepdims=True)
    result = (inner.T[:classes] - 0.5 * energy) / BAND
    for k in range(groups):
        at = (lax.axis_index("grp") ^ k) * own
        if own % TILE == 0:
            out[pl.ds(pl.multiple_of(at, TILE), own), :] = result[k * own : (k + 1) * own]
        else:
            for j in range(own):
                out[pl.ds(at + j, 1), :] = result[k * own + j : k * own + j + 1]


def swap(array, axis, flip):
    size = lax.axis_size(axis)
    return lax.ppermute(array, axis, [(i, i ^ flip) for i in range(size)])


def hop(array, near, groups):
    both = lax.axis_size("dp") * groups
    return lax.ppermute(
        array,
        ("dp", "grp"),
        [(i, i ^ ((near & 1) * groups | (near >> 1) * 2)) for i in range(both)],
    )


def body(images, shifts, class_ids, next_block):
    dp_count, groups = lax.axis_size("dp"), lax.axis_size("grp")
    own = CLASSES // (dp_count * groups)
    pairs = own // 2
    count = images.shape[0]
    nears, fars = groups, dp_count // 2
    block_rows = pairs * BAND + PACK
    vmem = pl.BlockSpec(memory_space=pltpu.VMEM)
    hbm = pl.BlockSpec(memory_space=pltpu.HBM)
    anywhere = pl.BlockSpec(memory_space=pl.ANY)
    flat = BAND * BAND
    spans = flat // PIX
    fresh_count = next_block.shape[0]

    def put(space, *arrays):
        return [pltpu.with_memory_space_constraint(a, space) for a in arrays]

    acc = pl.pallas_call(
        sums_kernel,
        out_shape=pltpu.VMEM((CLASSES * SLAB, PIX), jnp.float32),
        in_specs=[hbm] * 3,
        out_specs=vmem,
        scratch_shapes=[
            pltpu.VMEM((RING, CHUNK, PIX, PIX), jnp.bfloat16),
            pltpu.SMEM((count,), jnp.int32),
            pltpu.SMEM((2, count), jnp.int32),
            pltpu.SemaphoreType.DMA((RING,)),
            pltpu.SemaphoreType.DMA((2,)),
        ],
        compiler_params=pltpu.CompilerParams(vmem_limit_bytes=10 * MIB),
    )(*put(pltpu.HBM, class_ids, shifts.T, images))
    half = fars // 2
    piece = jax.ShapeDtypeStruct((2 * half, block_rows, PIX), jnp.bfloat16)
    ids_rows = class_ids.reshape(count // PIX, PIX)
    tables = [jnp.asarray(t) for t in (column_table(), row_table(), last_table(pairs))]

    (block,) = put(pltpu.HBM, next_block)
    (held_acc,) = put(pltpu.VMEM, acc)

    def transform(after, jobs, other):
        return pl.pallas_call(
            functools.partial(transform_kernel, jobs=jobs, other=other, groups=groups, own=own),
            out_shape=piece,
            in_specs=[anywhere] + [vmem] * 5,
            out_specs=vmem,
            scratch_shapes=[pltpu.VMEM((4, PACK, PIX), jnp.float32)],
            compiler_params=pltpu.CompilerParams(vmem_limit_bytes=8 * MIB),
            cost_estimate=pl.CostEstimate(flops=10**10, bytes_accessed=MIB, transcendentals=0),
        )(after, held_acc, ids_rows, *tables)

    met = {half: [], 0: []}
    done = ids_rows
    for first in (half, 0):
        for nears_here in ((3, 2), (1, 0)):
            jobs = tuple((near, first) for near in nears_here)
            send = transform(done, jobs, 1)
            got = swap(send, "grp", 1)
            keep = transform(send, jobs, 0)
            for k, near in enumerate(nears_here):
                span = slice(k * half, (k + 1) * half)
                part = keep[span].astype(jnp.float32) + got[span].astype(jnp.float32)
                part = part.astype(jnp.bfloat16)
                met[first].append(hop(part, near, groups) if near else part)
            done = part
    pieces = [None] * fars
    for first in (half, 0):
        totals = pl.pallas_call(
            functools.partial(totals_kernel, parts=nears),
            out_shape=[jax.ShapeDtypeStruct((block_rows, PIX), jnp.bfloat16)] * half,
            in_specs=[anywhere] + [vmem] * nears,
            out_specs=[vmem] * half,
            compiler_params=pltpu.CompilerParams(vmem_limit_bytes=8 * MIB),
        )(done, *met[first])
        for r, total in enumerate(totals):
            far = first + r
            pieces[far] = swap(total, "dp", far << 1) if far else total
        if first:
            fresh = pl.pallas_call(
                regroup_kernel,
                out_shape=pltpu.VMEM((spans, fresh_count, 2, PIX), jnp.bfloat16),
                in_specs=[anywhere, hbm],
                out_specs=vmem,
                scratch_shapes=[pltpu.SemaphoreType.DMA((spans,))],
                compiler_params=pltpu.CompilerParams(vmem_limit_bytes=8 * MIB),
                cost_estimate=pl.CostEstimate(flops=10**8, bytes_accessed=MIB, transcendentals=0),
            )(totals[0], block)
            done = fresh
    summed = pl.pallas_call(
        added_kernel,
        out_shape=jax.ShapeDtypeStruct((block_rows, PIX), jnp.bfloat16),
        in_specs=[vmem] * fars,
        out_specs=vmem,
        compiler_params=pltpu.CompilerParams(vmem_limit_bytes=8 * MIB),
    )(*put(pltpu.VMEM, *pieces))
    final_tables = jnp.asarray(expand_table()), jnp.asarray(filter_table())
    spread_scratch = [
        pltpu.VMEM((TILE * BAND, PIX), jnp.float32),
        pltpu.VMEM(((BAND + 1) * TILE, PIX), jnp.float32),
    ]
    averages, rounded = pl.pallas_call(
        functools.partial(averages_kernel, own=own, parts=fars),
        out_shape=(
            jax.ShapeDtypeStruct((own, 2, flat), jnp.float32),
            jax.ShapeDtypeStruct((TILE, 2 * flat), jnp.bfloat16),
        ),
        in_specs=[vmem] * (fars + 2),
        out_specs=(vmem, vmem),
        scratch_shapes=spread_scratch,
        compiler_params=pltpu.CompilerParams(vmem_limit_bytes=8 * MIB),
    )(*put(pltpu.VMEM, *pieces), *final_tables)

    def references(after, piece):
        return pl.pallas_call(
            functools.partial(references_kernel, own=own),
            out_shape=jax.ShapeDtypeStruct((TILE, 2 * flat), jnp.bfloat16),
            in_specs=[anywhere] + [vmem] * 3,
            out_specs=vmem,
            scratch_shapes=spread_scratch,
            compiler_params=pltpu.CompilerParams(vmem_limit_bytes=8 * MIB),
            cost_estimate=pl.CostEstimate(flops=10**10, bytes_accessed=MIB, transcendentals=0),
        )(after, *put(pltpu.VMEM, piece), *final_tables)

    held = [rounded, references(rounded, swap(summed, "grp", 1))]
    for k in range(2, groups, 2):
        across = swap(summed, "grp", k)
        held.append(references(held[-1], across))
        held.append(references(held[-1], swap(across, "grp", 1)))
    fresh = [fresh.reshape(spans, 2 * fresh_count, PIX)]
    scores = pl.pallas_call(
        functools.partial(scores_kernel, own=own, groups=groups),
        out_shape=jax.ShapeDtypeStruct((own * groups, fresh_count), jnp.float32),
        in_specs=[vmem] * (groups + len(fresh)),
        out_specs=vmem,
        scratch_shapes=[pltpu.VMEM((2 * fresh_count, PIX), jnp.float32)],
        compiler_params=pltpu.CompilerParams(vmem_limit_bytes=16 * MIB),
    )(*put(pltpu.VMEM, *held, *fresh))
    return averages, scores


def solution(mesh):
    placed = (
        P(("dp", "grp"), None, None),
        P(("dp", "grp"), None),
        P(("dp", "grp")),
        P("grp", None, None),
    )
    return jax.shard_map(
        body,
        mesh=mesh,
        in_specs=placed,
        out_specs=(P(("dp", "grp"), None, None), P("dp", "grp")),
        check_vma=False,
    )
```

```python
import functools
import math

import jax
import jax.numpy as jnp
import ml_dtypes
import numpy as np
from jax import lax
from jax.experimental import pallas as pl
from jax.experimental.pallas import tpu as pltpu
from jax.sharding import PartitionSpec as P

PIX = 128
BAND = 64
CLASSES = 256
HALF = BAND // 2
RIDGE = 4.0
REACH = 16
SLAB = PIX + 2 * REACH
TILE = 8
PACK = 16
ROWS = BAND + PACK
DIGITS = 4
CHUNK = 32
RING = 6
UNROLL = 32
MIB = 1 << 20


def basis():
    position = np.arange(PIX)
    freq = np.concatenate([np.arange(HALF + 1), np.arange(1, HALF + 1)])
    angle = (position[:, None] * freq[None, :] % PIX) * (2.0 * math.pi / PIX)
    is_cos = np.arange(BAND + 1) <= HALF
    table = np.where(is_cos[None, :], np.cos(angle), np.sin(angle)) / math.sqrt(PIX)
    return table.astype(np.float32).astype(ml_dtypes.bfloat16)


def column_table():
    table = basis()
    out = np.zeros((2 * PIX, PIX), ml_dtypes.bfloat16)
    for side in range(2):
        out[side * PIX : (side + 1) * PIX, side * BAND : (side + 1) * BAND] = table[:, :BAND]
    return out


def last_table(pairs):
    table = basis()
    out = np.zeros((PACK, pairs, 2 * PIX), ml_dtypes.bfloat16)
    for j in range(pairs):
        for side in range(2):
            out[j + side * pairs, j, side * PIX : (side + 1) * PIX] = table[:, BAND]
    return out.reshape(PACK, -1)


def row_table():
    out = np.zeros((ROWS, PIX), ml_dtypes.bfloat16)
    out[: BAND + 1] = basis().T
    return out


def expand_table():
    out = np.zeros((PIX, 2 * PIX), ml_dtypes.bfloat16)
    for at in range(BAND):
        k = at - HALF
        for copy in range(2):
            out[abs(k), copy * BAND + at] = 1.0
            if k:
                row = BAND if abs(k) == HALF else HALF + abs(k)
                out[row, PIX + copy * BAND + at] = math.copysign(1.0, k)
    return out


def filter_table():
    squared = (np.arange(BAND, dtype=np.float32) - HALF) ** 2
    radius = squared[:, None] + squared[None, :]
    return np.exp(-radius / (BAND * BAND / 2.0)).reshape(BAND // 2, 2 * BAND).astype(np.float32)


def owner_of(near, far, other, groups):
    dp, grp = lax.axis_index("dp"), lax.axis_index("grp")
    there_dp = dp ^ ((far << 1) | (near & 1))
    there_grp = grp ^ (((near >> 1) << 1) | other)
    return there_dp * groups + there_grp


def sums_kernel(
    class_ids, pixel_shifts, images, acc, held, ids, shifts, sems, small_sem
):
    chunks = images.shape[0] // CHUNK

    def fetch(k):
        span = pl.ds(pl.multiple_of(k * CHUNK, CHUNK), CHUNK)
        slot = lax.rem(k, RING)
        return pltpu.make_async_copy(images.at[span], held.at[slot], sems.at[slot])

    small = [
        pltpu.make_async_copy(class_ids, ids, small_sem.at[0]),
        pltpu.make_async_copy(pixel_shifts, shifts, small_sem.at[1]),
    ]
    for copy in small:
        copy.start()
    for k in range(min(RING, chunks)):
        fetch(k).start()
    acc[...] = jnp.zeros_like(acc)
    for copy in small:
        copy.wait()

    def add_chunk(k, _):
        fetch(k).wait()
        slot = lax.rem(k, RING)

        def add_some(s, _):
            for u in range(UNROLL):
                i = k * CHUNK + s * UNROLL + u
                dx = shifts[0, i]
                at = ids[i] * SLAB + REACH + shifts[1, i]
                turned = pltpu.roll(
                    held[slot, s * UNROLL + u].astype(jnp.float32), jnp.where(dx < 0, dx + PIX, dx), 1
                )
                acc[pl.ds(at, PIX), :] = acc[pl.ds(at, PIX), :] + turned
            return 0

        lax.fori_loop(0, CHUNK // UNROLL, add_some, 0)

        @pl.when(k + RING < chunks)
        def _():
            fetch(k + RING).start()

        return 0

    lax.fori_loop(0, chunks, add_chunk, 0)


def transform_kernel(
    _, acc, ids_rows, col, row, last, out, edges, *, jobs, other, groups, own
):
    pairs = own // 2
    count = out.shape[0]
    half = count // len(jobs)
    together = 4 if count % 4 == 0 else 1
    lane = lax.broadcasted_iota(jnp.int32, (TILE, ROWS), 1)
    sub = lax.broadcasted_iota(jnp.int32, (TILE, PIX), 0)
    edges[...] = jnp.zeros_like(edges)

    def folded(c):
        at = pl.multiple_of(c * SLAB, TILE)
        head = acc[pl.ds(at + REACH, REACH), :] + acc[pl.ds(at + PIX + REACH, REACH), :]
        mid = acc[pl.ds(at + 2 * REACH, PIX - 2 * REACH), :]
        tail = acc[pl.ds(at + PIX, REACH), :] + acc[pl.ds(at, REACH), :]
        return jnp.concatenate([head, mid, tail], axis=0).astype(jnp.bfloat16)

    def transform(far, edge):
        near, first = jobs[-1]
        which = lax.div(far, half)
        for k, job in enumerate(jobs[:-1]):
            near = jnp.where(which == k, job[0], near)
            first = jnp.where(which == k, job[1], first)
        owner = owner_of(near, first + lax.rem(far, half), other, groups)
        wide = jnp.concatenate(
            [folded(owner * own + j + side * pairs) for j in range(pairs) for side in range(2)], axis=1
        )
        part = jnp.dot(row[...], wide, preferred_element_type=jnp.float32).astype(jnp.bfloat16)
        ends = lax.dot_general(
            last[...], part, (((1,), (1,)), ((), ())), preferred_element_type=jnp.float32
        )
        full = jnp.dot(
            jnp.concatenate(
                [part[:, 2 * PIX * j : 2 * PIX * (j + 1)] for j in range(pairs)], axis=0
            ),
            col[...],
            preferred_element_type=jnp.float32,
        )
        for j in range(pairs):
            at = j * ROWS
            out[far, j * BAND : (j + 1) * BAND, :] = full[at : at + BAND].astype(jnp.bfloat16)
            edge[j : j + 1, :] = full[at + BAND : at + BAND + 1]
        hits = jnp.zeros((TILE, PIX), jnp.float32)
        for r in range(ids_rows.shape[0]):
            hits += (ids_rows[r : r + 1, :] == owner * own + sub).astype(jnp.float32)
        rest = jnp.sum(hits, axis=1, keepdims=True)
        ends = ends[:TILE]
        for d in range(DIGITS):
            upper = jnp.floor(rest * 0.125) if d < DIGITS - 1 else jnp.zeros_like(rest)
            ends = jnp.where(lane == BAND + 1 + d, rest - 8.0 * upper, ends)
            rest = upper
        edge[TILE:, :ROWS] = ends
        out[far, pairs * BAND :, :] = edge[...].astype(jnp.bfloat16)

    def some(n, _):
        for k in range(together):
            transform(n * together + k, edges.at[k])
        return 0

    lax.fori_loop(0, count // together, some, 0)


def regroup_kernel(_, block, fresh, sems, *, first):
    copies = [
        pltpu.make_async_copy(
            block.at[:, :, pl.ds((first + f) * PIX, PIX)], fresh.at[f], sems.at[f]
        )
        for f in range(fresh.shape[0])
    ]
    for copy in copies:
        copy.start()
    for copy in copies:
        copy.wait()


def totals_kernel(_, *refs, parts):
    for r, out in enumerate(refs[parts:]):
        total = refs[0][r].astype(jnp.float32)
        for ref in refs[1:parts]:
            total += ref[r].astype(jnp.float32)
        out[...] = total.astype(jnp.bfloat16)


def added(pieces):
    total = pieces[0][...].astype(jnp.float32)
    for piece in pieces[1:]:
        total += piece[...].astype(jnp.float32)
    return total


def added_kernel(_, *refs):
    refs[-1][...] = added(refs[:-1]).astype(jnp.bfloat16)


def averages_kernel(*refs, own, parts):
    pieces, (expand, taper, out, rounded, wide, rows) = refs[:parts], refs[parts:]

    def emit(u, part, value):
        out[:, part, u * PIX : (u + 1) * PIX] = value[:own]
        at = part * BAND * BAND + u * PIX
        rounded[:, at : at + PIX] = value.astype(jnp.bfloat16)

    spread_out(added(pieces), 3, expand, taper, wide, rows, own, emit)


def references_kernel(*refs, own):
    _, piece, expand, taper, rounded, wide, rows = refs

    def emit(u, part, value):
        at = part * BAND * BAND + u * PIX
        rounded[:, at : at + PIX] = value.astype(jnp.bfloat16)

    spread_out(piece[...].astype(jnp.float32), 1, expand, taper, wide, rows, own, emit)


def spread_out(total, pieces, expand, taper, wide, rows, own, emit):
    pairs = own // 2
    main, ends = total[: pairs * BAND], total[pairs * BAND :]
    if own < TILE:
        wide[...] = jnp.zeros_like(wide)
    wide[: pairs * BAND, :] = main
    wide[pairs * BAND : 2 * pairs * BAND, :] = pltpu.roll(main, BAND, 1)
    extra = ends[TILE:]
    lane = lax.broadcasted_iota(jnp.int32, (TILE, PIX), 1)
    for t in range(BAND + 1):
        if t < BAND:
            line = wide[pl.ds(t, TILE, stride=BAND), :]
        else:
            edge = ends[:pairs]
            line = jnp.concatenate([edge, pltpu.roll(ends[:TILE], BAND, 1)[:pairs]], axis=0)
            if own < TILE:
                line = jnp.concatenate([line, jnp.zeros((TILE - own, PIX), jnp.float32)], axis=0)
        line = jnp.where(
            lane < BAND, line, jnp.where(lane == BAND, extra[:, t : t + 1], 0.0)
        )
        rows[t * TILE : (t + 1) * TILE, :] = line
    spread = None
    rest = rows[...]
    for k in range(pieces):
        here = rest.astype(jnp.bfloat16)
        rest = rest - here.astype(jnp.float32) if k + 1 < pieces else None
        term = jnp.dot(here, expand[...], preferred_element_type=jnp.float32)
        spread = term if spread is None else spread + term

    def cos_part(t):
        return spread[t * TILE : (t + 1) * TILE, :PIX]

    def sin_part(t):
        return spread[t * TILE : (t + 1) * TILE, PIX:]

    members = jnp.zeros((TILE, 1), jnp.float32)
    for d in range(DIGITS):
        members += extra[:, BAND + 1 + d : BAND + 2 + d] * float(8**d)
    weight = members + RIDGE

    def at_frequency(k):
        c = abs(k)
        if k == 0:
            return cos_part(0), -sin_part(0)
        s = BAND if c == HALF else HALF + c
        if k > 0:
            return cos_part(c) - sin_part(s), -(cos_part(s) + sin_part(c))
        return cos_part(c) + sin_part(s), cos_part(s) - sin_part(c)

    for u in range(BAND // 2):
        even, odd = at_frequency(2 * u - HALF), at_frequency(2 * u + 1 - HALF)
        for part in range(2):
            value = jnp.where(lane < BAND, even[part], odd[part]) * taper[u : u + 1, :] / weight
            emit(u, part, value)


def scores_kernel(*refs, own, groups):
    pieces, fresh, (out, sums) = refs[:groups], refs[groups:-2], refs[-2:]
    each = fresh[0].shape[0]
    spans = len(fresh) * each
    classes = own * groups
    held = jnp.concatenate([piece[:own] for piece in pieces], axis=0)
    both = jnp.concatenate([held[:, : spans * PIX], held[:, spans * PIX :]], axis=0)
    total = None
    for f in range(0, spans, 2):
        here = jnp.concatenate([fresh[g // each][g % each] for g in (f, f + 1)], axis=1)
        term = lax.dot_general(
            here,
            both[:, f * PIX : (f + 2) * PIX],
            (((1,), (1,)), ((), ())),
            preferred_element_type=jnp.float32,
        )
        total = term if total is None else total + term
    sums[:, : 2 * classes] = total
    count = out.shape[1]
    inner = sums[pl.ds(0, count, stride=2), :] + pltpu.roll(
        sums[pl.ds(1, count, stride=2), :], PIX - classes, 1
    )
    energy = jnp.sum(jnp.square(held.astype(jnp.float32)), axis=1, keepdims=True)
    result = (inner.T[:classes] - 0.5 * energy) / BAND
    for k in range(groups):
        at = (lax.axis_index("grp") ^ k) * own
        if own % TILE == 0:
            out[pl.ds(pl.multiple_of(at, TILE), own), :] = result[k * own : (k + 1) * own]
        else:
            for j in range(own):
                out[pl.ds(at + j, 1), :] = result[k * own + j : k * own + j + 1]


def swap(array, axis, flip):
    size = lax.axis_size(axis)
    return lax.ppermute(array, axis, [(i, i ^ flip) for i in range(size)])


def hop(array, near, groups):
    both = lax.axis_size("dp") * groups
    return lax.ppermute(
        array,
        ("dp", "grp"),
        [(i, i ^ ((near & 1) * groups | (near >> 1) * 2)) for i in range(both)],
    )


def body(images, shifts, class_ids, next_block):
    dp_count, groups = lax.axis_size("dp"), lax.axis_size("grp")
    own = CLASSES // (dp_count * groups)
    pairs = own // 2
    count = images.shape[0]
    nears, fars = groups, dp_count // 2
    block_rows = pairs * BAND + PACK
    vmem = pl.BlockSpec(memory_space=pltpu.VMEM)
    hbm = pl.BlockSpec(memory_space=pltpu.HBM)
    anywhere = pl.BlockSpec(memory_space=pl.ANY)
    flat = BAND * BAND
    spans = flat // PIX // 2
    fresh_count = next_block.shape[0]

    def put(space, *arrays):
        return [pltpu.with_memory_space_constraint(a, space) for a in arrays]

    acc = pl.pallas_call(
        sums_kernel,
        out_shape=pltpu.VMEM((CLASSES * SLAB, PIX), jnp.float32),
        in_specs=[hbm] * 3,
        out_specs=vmem,
        scratch_shapes=[
            pltpu.VMEM((RING, CHUNK, PIX, PIX), jnp.bfloat16),
            pltpu.SMEM((count,), jnp.int32),
            pltpu.SMEM((2, count), jnp.int32),
            pltpu.SemaphoreType.DMA((RING,)),
            pltpu.SemaphoreType.DMA((2,)),
        ],
        compiler_params=pltpu.CompilerParams(vmem_limit_bytes=10 * MIB),
    )(*put(pltpu.HBM, class_ids, shifts.T, images))
    half = fars // 2
    piece = jax.ShapeDtypeStruct((2 * half, block_rows, PIX), jnp.bfloat16)
    ids_rows = class_ids.reshape(count // PIX, PIX)
    tables = [jnp.asarray(t) for t in (column_table(), row_table(), last_table(pairs))]

    (block,) = put(pltpu.HBM, next_block)
    (held_acc,) = put(pltpu.VMEM, acc)

    def transform(after, jobs, other):
        return pl.pallas_call(
            functools.partial(transform_kernel, jobs=jobs, other=other, groups=groups, own=own),
            out_shape=piece,
            in_specs=[anywhere] + [vmem] * 5,
            out_specs=vmem,
            scratch_shapes=[pltpu.VMEM((4, PACK, PIX), jnp.float32)],
            compiler_params=pltpu.CompilerParams(vmem_limit_bytes=8 * MIB),
            cost_estimate=pl.CostEstimate(flops=10**10, bytes_accessed=MIB, transcendentals=0),
        )(after, held_acc, ids_rows, *tables)

    met = {half: [], 0: []}
    done = ids_rows
    for first in (half, 0):
        for nears_here in ((3, 2), (1, 0)):
            jobs = tuple((near, first) for near in nears_here)
            send = transform(done, jobs, 1)
            got = swap(send, "grp", 1)
            keep = transform(send, jobs, 0)
            for k, near in enumerate(nears_here):
                span = slice(k * half, (k + 1) * half)
                part = keep[span].astype(jnp.float32) + got[span].astype(jnp.float32)
                part = part.astype(jnp.bfloat16)
                met[first].append(hop(part, near, groups) if near else part)
            done = part
    def regroup(after, first):
        return pl.pallas_call(
            functools.partial(regroup_kernel, first=first),
            out_shape=pltpu.VMEM((spans, fresh_count, 2, PIX), jnp.bfloat16),
            in_specs=[anywhere, hbm],
            out_specs=vmem,
            scratch_shapes=[pltpu.SemaphoreType.DMA((spans,))],
            compiler_params=pltpu.CompilerParams(vmem_limit_bytes=8 * MIB),
            cost_estimate=pl.CostEstimate(flops=10**8, bytes_accessed=MIB, transcendentals=0),
        )(after, block)

    fresh = []
    pieces = [None] * fars
    for first in (half, 0):
        totals = pl.pallas_call(
            functools.partial(totals_kernel, parts=nears),
            out_shape=[jax.ShapeDtypeStruct((block_rows, PIX), jnp.bfloat16)] * half,
            in_specs=[anywhere] + [vmem] * nears,
            out_specs=[vmem] * half,
            compiler_params=pltpu.CompilerParams(vmem_limit_bytes=8 * MIB),
        )(done, *met[first])
        for r, total in enumerate(totals):
            far = first + r
            pieces[far] = swap(total, "dp", far << 1) if far else total
        done = regroup(totals[0], len(fresh) * spans)
        fresh.append(done)
    summed = pl.pallas_call(
        added_kernel,
        out_shape=jax.ShapeDtypeStruct((block_rows, PIX), jnp.bfloat16),
        in_specs=[anywhere] + [vmem] * fars,
        out_specs=vmem,
        compiler_params=pltpu.CompilerParams(vmem_limit_bytes=8 * MIB),
    )(done, *put(pltpu.VMEM, *pieces))
    final_tables = jnp.asarray(expand_table()), jnp.asarray(filter_table())
    spread_scratch = [
        pltpu.VMEM((TILE * BAND, PIX), jnp.float32),
        pltpu.VMEM(((BAND + 1) * TILE, PIX), jnp.float32),
    ]
    averages, rounded = pl.pallas_call(
        functools.partial(averages_kernel, own=own, parts=fars),
        out_shape=(
            jax.ShapeDtypeStruct((own, 2, flat), jnp.float32),
            jax.ShapeDtypeStruct((TILE, 2 * flat), jnp.bfloat16),
        ),
        in_specs=[vmem] * (fars + 2),
        out_specs=(vmem, vmem),
        scratch_shapes=spread_scratch,
        compiler_params=pltpu.CompilerParams(vmem_limit_bytes=8 * MIB),
    )(*put(pltpu.VMEM, *pieces), *final_tables)

    def references(after, piece):
        return pl.pallas_call(
            functools.partial(references_kernel, own=own),
            out_shape=jax.ShapeDtypeStruct((TILE, 2 * flat), jnp.bfloat16),
            in_specs=[anywhere] + [vmem] * 3,
            out_specs=vmem,
            scratch_shapes=spread_scratch,
            compiler_params=pltpu.CompilerParams(vmem_limit_bytes=8 * MIB),
            cost_estimate=pl.CostEstimate(flops=10**10, bytes_accessed=MIB, transcendentals=0),
        )(after, *put(pltpu.VMEM, piece), *final_tables)

    held = [rounded, references(rounded, swap(summed, "grp", 1))]
    for k in range(2, groups, 2):
        across = swap(summed, "grp", k)
        held.append(references(held[-1], across))
        held.append(references(held[-1], swap(across, "grp", 1)))
    fresh = [f.reshape(spans, 2 * fresh_count, PIX) for f in fresh]
    scores = pl.pallas_call(
        functools.partial(scores_kernel, own=own, groups=groups),
        out_shape=jax.ShapeDtypeStruct((own * groups, fresh_count), jnp.float32),
        in_specs=[vmem] * (groups + len(fresh)),
        out_specs=vmem,
        scratch_shapes=[pltpu.VMEM((2 * fresh_count, PIX), jnp.float32)],
        compiler_params=pltpu.CompilerParams(vmem_limit_bytes=16 * MIB),
    )(*put(pltpu.VMEM, *held, *fresh))
    return averages, scores


def solution(mesh):
    placed = (
        P(("dp", "grp"), None, None),
        P(("dp", "grp"), None),
        P(("dp", "grp")),
        P("grp", None, None),
    )
    return jax.shard_map(
        body,
        mesh=mesh,
        in_specs=placed,
        out_specs=(P(("dp", "grp"), None, None), P("dp", "grp")),
        check_vma=False,
    )
```

```python
import functools
import math

import jax
import jax.numpy as jnp
import ml_dtypes
import numpy as np
from jax import lax
from jax.experimental import pallas as pl
from jax.experimental.pallas import tpu as pltpu
from jax.sharding import PartitionSpec as P

PIX = 128
BAND = 64
CLASSES = 256
HALF = BAND // 2
RIDGE = 4.0
REACH = 16
SLAB = PIX + 2 * REACH
TILE = 8
PACK = 16
ROWS = BAND + PACK
DIGITS = 4
CHUNK = 32
RING = 6
UNROLL = 32
MIB = 1 << 20


def basis():
    position = np.arange(PIX)
    freq = np.concatenate([np.arange(HALF + 1), np.arange(1, HALF + 1)])
    angle = (position[:, None] * freq[None, :] % PIX) * (2.0 * math.pi / PIX)
    is_cos = np.arange(BAND + 1) <= HALF
    table = np.where(is_cos[None, :], np.cos(angle), np.sin(angle)) / math.sqrt(PIX)
    return table.astype(np.float32).astype(ml_dtypes.bfloat16)


def column_table():
    table = basis()
    out = np.zeros((2 * PIX, PIX), ml_dtypes.bfloat16)
    for side in range(2):
        out[side * PIX : (side + 1) * PIX, side * BAND : (side + 1) * BAND] = table[:, :BAND]
    return out


def last_table(pairs):
    table = basis()
    out = np.zeros((PACK, pairs, 2 * PIX), ml_dtypes.bfloat16)
    for j in range(pairs):
        for side in range(2):
            out[j + side * pairs, j, side * PIX : (side + 1) * PIX] = table[:, BAND]
    return out.reshape(PACK, -1)


def row_table():
    out = np.zeros((ROWS, PIX), ml_dtypes.bfloat16)
    out[: BAND + 1] = basis().T
    return out


def expand_table():
    out = np.zeros((PIX, 2 * PIX), ml_dtypes.bfloat16)
    for at in range(BAND):
        k = at - HALF
        for copy in range(2):
            out[abs(k), copy * BAND + at] = 1.0
            if k:
                row = BAND if abs(k) == HALF else HALF + abs(k)
                out[row, PIX + copy * BAND + at] = math.copysign(1.0, k)
    return out


def filter_table():
    squared = (np.arange(BAND, dtype=np.float32) - HALF) ** 2
    radius = squared[:, None] + squared[None, :]
    return np.exp(-radius / (BAND * BAND / 2.0)).reshape(BAND // 2, 2 * BAND).astype(np.float32)


def owner_of(near, far, other, groups):
    dp, grp = lax.axis_index("dp"), lax.axis_index("grp")
    there_dp = dp ^ ((far << 1) | (near & 1))
    there_grp = grp ^ (((near >> 1) << 1) | other)
    return there_dp * groups + there_grp


def sums_kernel(
    class_ids, pixel_shifts, images, acc, held, ids, shifts, sems, small_sem
):
    chunks = images.shape[0] // CHUNK

    def fetch(k):
        span = pl.ds(pl.multiple_of(k * CHUNK, CHUNK), CHUNK)
        slot = lax.rem(k, RING)
        return pltpu.make_async_copy(images.at[span], held.at[slot], sems.at[slot])

    small = [
        pltpu.make_async_copy(class_ids, ids, small_sem.at[0]),
        pltpu.make_async_copy(pixel_shifts, shifts, small_sem.at[1]),
    ]
    for copy in small:
        copy.start()
    for k in range(min(RING, chunks)):
        fetch(k).start()
    acc[...] = jnp.zeros_like(acc)
    for copy in small:
        copy.wait()

    def add_chunk(k, _):
        fetch(k).wait()
        slot = lax.rem(k, RING)

        def add_some(s, _):
            for u in range(UNROLL):
                i = k * CHUNK + s * UNROLL + u
                dx = shifts[0, i]
                at = ids[i] * SLAB + REACH + shifts[1, i]
                turned = pltpu.roll(
                    held[slot, s * UNROLL + u].astype(jnp.float32), jnp.where(dx < 0, dx + PIX, dx), 1
                )
                acc[pl.ds(at, PIX), :] = acc[pl.ds(at, PIX), :] + turned
            return 0

        lax.fori_loop(0, CHUNK // UNROLL, add_some, 0)

        @pl.when(k + RING < chunks)
        def _():
            fetch(k + RING).start()

        return 0

    lax.fori_loop(0, chunks, add_chunk, 0)


def transform_kernel(
    _, acc, ids_rows, col, row, last, out, edges, *, jobs, other, groups, own
):
    pairs = own // 2
    count = out.shape[0]
    half = count // len(jobs)
    together = 4 if count % 4 == 0 else 1
    lane = lax.broadcasted_iota(jnp.int32, (TILE, ROWS), 1)
    sub = lax.broadcasted_iota(jnp.int32, (TILE, PIX), 0)
    edges[...] = jnp.zeros_like(edges)

    def folded(c):
        at = pl.multiple_of(c * SLAB, TILE)
        head = acc[pl.ds(at + REACH, REACH), :] + acc[pl.ds(at + PIX + REACH, REACH), :]
        mid = acc[pl.ds(at + 2 * REACH, PIX - 2 * REACH), :]
        tail = acc[pl.ds(at + PIX, REACH), :] + acc[pl.ds(at, REACH), :]
        return jnp.concatenate([head, mid, tail], axis=0).astype(jnp.bfloat16)

    def transform(far, edge):
        near, first = jobs[-1]
        which = lax.div(far, half)
        for k, job in enumerate(jobs[:-1]):
            near = jnp.where(which == k, job[0], near)
            first = jnp.where(which == k, job[1], first)
        owner = owner_of(near, first + lax.rem(far, half), other, groups)
        wide = jnp.concatenate(
            [folded(owner * own + j + side * pairs) for j in range(pairs) for side in range(2)], axis=1
        )
        part = jnp.dot(row[...], wide, preferred_element_type=jnp.float32).astype(jnp.bfloat16)
        ends = lax.dot_general(
            last[...], part, (((1,), (1,)), ((), ())), preferred_element_type=jnp.float32
        )
        full = jnp.dot(
            jnp.concatenate(
                [part[:, 2 * PIX * j : 2 * PIX * (j + 1)] for j in range(pairs)], axis=0
            ),
            col[...],
            preferred_element_type=jnp.float32,
        )
        for j in range(pairs):
            at = j * ROWS
            out[far, j * BAND : (j + 1) * BAND, :] = full[at : at + BAND].astype(jnp.bfloat16)
            edge[j : j + 1, :] = full[at + BAND : at + BAND + 1]
        hits = jnp.zeros((TILE, PIX), jnp.float32)
        for r in range(ids_rows.shape[0]):
            hits += (ids_rows[r : r + 1, :] == owner * own + sub).astype(jnp.float32)
        rest = jnp.sum(hits, axis=1, keepdims=True)
        ends = ends[:TILE]
        for d in range(DIGITS):
            upper = jnp.floor(rest * 0.125) if d < DIGITS - 1 else jnp.zeros_like(rest)
            ends = jnp.where(lane == BAND + 1 + d, rest - 8.0 * upper, ends)
            rest = upper
        edge[TILE:, :ROWS] = ends
        out[far, pairs * BAND :, :] = edge[...].astype(jnp.bfloat16)

    def some(n, _):
        for k in range(together):
            transform(n * together + k, edges.at[k])
        return 0

    lax.fori_loop(0, count // together, some, 0)


def regroup_kernel(_, block, fresh, sems, *, first):
    copies = [
        pltpu.make_async_copy(
            block.at[:, :, pl.ds((first + f) * PIX, PIX)], fresh.at[f], sems.at[f]
        )
        for f in range(fresh.shape[0])
    ]
    for copy in copies:
        copy.start()
    for copy in copies:
        copy.wait()


def totals_kernel(_, *refs, parts):
    for r, out in enumerate(refs[parts:]):
        total = refs[0][r].astype(jnp.float32)
        for ref in refs[1:parts]:
            total += ref[r].astype(jnp.float32)
        out[...] = total.astype(jnp.bfloat16)


def added(pieces):
    total = pieces[0][...].astype(jnp.float32)
    for piece in pieces[1:]:
        total += piece[...].astype(jnp.float32)
    return total


def added_kernel(_, *refs):
    refs[-1][...] = added(refs[:-1]).astype(jnp.bfloat16)


def averages_kernel(*refs, own, parts):
    pieces, (expand, taper, out, rounded, wide, rows) = refs[:parts], refs[parts:]

    def emit(u, part, value):
        out[:, part, u * PIX : (u + 1) * PIX] = value[:own]
        at = part * BAND * BAND + u * PIX
        rounded[:, at : at + PIX] = value.astype(jnp.bfloat16)

    spread_out(added(pieces), 3, expand, taper, wide, rows, own, emit)


def references_kernel(*refs, own):
    _, piece, expand, taper, rounded, wide, rows = refs

    def emit(u, part, value):
        at = part * BAND * BAND + u * PIX
        rounded[:, at : at + PIX] = value.astype(jnp.bfloat16)

    spread_out(piece[...].astype(jnp.float32), 1, expand, taper, wide, rows, own, emit)


def spread_out(total, pieces, expand, taper, wide, rows, own, emit):
    pairs = own // 2
    main, ends = total[: pairs * BAND], total[pairs * BAND :]
    if own < TILE:
        wide[...] = jnp.zeros_like(wide)
    wide[: pairs * BAND, :] = main
    wide[pairs * BAND : 2 * pairs * BAND, :] = pltpu.roll(main, BAND, 1)
    extra = ends[TILE:]
    lane = lax.broadcasted_iota(jnp.int32, (TILE, PIX), 1)
    for t in range(BAND + 1):
        if t < BAND:
            line = wide[pl.ds(t, TILE, stride=BAND), :]
        else:
            edge = ends[:pairs]
            line = jnp.concatenate([edge, pltpu.roll(ends[:TILE], BAND, 1)[:pairs]], axis=0)
            if own < TILE:
                line = jnp.concatenate([line, jnp.zeros((TILE - own, PIX), jnp.float32)], axis=0)
        line = jnp.where(
            lane < BAND, line, jnp.where(lane == BAND, extra[:, t : t + 1], 0.0)
        )
        rows[t * TILE : (t + 1) * TILE, :] = line
    spread = None
    rest = rows[...]
    for k in range(pieces):
        here = rest.astype(jnp.bfloat16)
        rest = rest - here.astype(jnp.float32) if k + 1 < pieces else None
        term = jnp.dot(here, expand[...], preferred_element_type=jnp.float32)
        spread = term if spread is None else spread + term

    def cos_part(t):
        return spread[t * TILE : (t + 1) * TILE, :PIX]

    def sin_part(t):
        return spread[t * TILE : (t + 1) * TILE, PIX:]

    members = jnp.zeros((TILE, 1), jnp.float32)
    for d in range(DIGITS):
        members += extra[:, BAND + 1 + d : BAND + 2 + d] * float(8**d)
    weight = members + RIDGE

    def at_frequency(k):
        c = abs(k)
        if k == 0:
            return cos_part(0), -sin_part(0)
        s = BAND if c == HALF else HALF + c
        if k > 0:
            return cos_part(c) - sin_part(s), -(cos_part(s) + sin_part(c))
        return cos_part(c) + sin_part(s), cos_part(s) - sin_part(c)

    for u in range(BAND // 2):
        even, odd = at_frequency(2 * u - HALF), at_frequency(2 * u + 1 - HALF)
        for part in range(2):
            value = jnp.where(lane < BAND, even[part], odd[part]) * taper[u : u + 1, :] / weight
            emit(u, part, value)


def scores_kernel(*refs, own, groups):
    pieces, fresh, (out, sums) = refs[:groups], refs[groups:-2], refs[-2:]
    each = fresh[0].shape[0]
    spans = len(fresh) * each
    classes = own * groups
    held = jnp.concatenate([piece[:own] for piece in pieces], axis=0)
    both = jnp.concatenate([held[:, : spans * PIX], held[:, spans * PIX :]], axis=0)
    total = None
    for f in range(0, spans, 2):
        here = jnp.concatenate([fresh[g // each][g % each] for g in (f, f + 1)], axis=1)
        term = lax.dot_general(
            here,
            both[:, f * PIX : (f + 2) * PIX],
            (((1,), (1,)), ((), ())),
            preferred_element_type=jnp.float32,
        )
        total = term if total is None else total + term
    sums[: total.shape[0], : 2 * classes] = total
    count = out.shape[1]
    inner = sums[pl.ds(0, count, stride=2), :] + pltpu.roll(
        sums[pl.ds(1, count, stride=2), :], PIX - classes, 1
    )
    energy = jnp.sum(jnp.square(held.astype(jnp.float32)), axis=1, keepdims=True)
    result = (inner.T[:classes] - 0.5 * energy) / BAND
    for k in range(groups):
        at = (lax.axis_index("grp") ^ k) * own
        if own % TILE == 0:
            out[pl.ds(pl.multiple_of(at, TILE), own), :] = result[k * own : (k + 1) * own]
        else:
            for j in range(own):
                out[pl.ds(at + j, 1), :] = result[k * own + j : k * own + j + 1]


def swap(array, axis, flip):
    size = lax.axis_size(axis)
    return lax.ppermute(array, axis, [(i, i ^ flip) for i in range(size)])


def hop(array, near, groups):
    both = lax.axis_size("dp") * groups
    return lax.ppermute(
        array,
        ("dp", "grp"),
        [(i, i ^ ((near & 1) * groups | (near >> 1) * 2)) for i in range(both)],
    )


def body(images, shifts, class_ids, next_block):
    dp_count, groups = lax.axis_size("dp"), lax.axis_size("grp")
    own = CLASSES // (dp_count * groups)
    pairs = own // 2
    count = images.shape[0]
    nears, fars = groups, dp_count // 2
    block_rows = pairs * BAND + PACK
    vmem = pl.BlockSpec(memory_space=pltpu.VMEM)
    hbm = pl.BlockSpec(memory_space=pltpu.HBM)
    anywhere = pl.BlockSpec(memory_space=pl.ANY)
    flat = BAND * BAND
    spans = flat // PIX // 2
    fresh_count = next_block.shape[0]

    def put(space, *arrays):
        return [pltpu.with_memory_space_constraint(a, space) for a in arrays]

    acc = pl.pallas_call(
        sums_kernel,
        out_shape=pltpu.VMEM((CLASSES * SLAB, PIX), jnp.float32),
        in_specs=[hbm] * 3,
        out_specs=vmem,
        scratch_shapes=[
            pltpu.VMEM((RING, CHUNK, PIX, PIX), jnp.bfloat16),
            pltpu.SMEM((count,), jnp.int32),
            pltpu.SMEM((2, count), jnp.int32),
            pltpu.SemaphoreType.DMA((RING,)),
            pltpu.SemaphoreType.DMA((2,)),
        ],
        compiler_params=pltpu.CompilerParams(vmem_limit_bytes=10 * MIB),
    )(*put(pltpu.HBM, class_ids, shifts.T, images))
    half = fars // 2
    piece = jax.ShapeDtypeStruct((2 * half, block_rows, PIX), jnp.bfloat16)
    ids_rows = class_ids.reshape(count // PIX, PIX)
    tables = [jnp.asarray(t) for t in (column_table(), row_table(), last_table(pairs))]

    (block,) = put(pltpu.HBM, next_block)
    (held_acc,) = put(pltpu.VMEM, acc)

    def transform(after, jobs, other):
        return pl.pallas_call(
            functools.partial(transform_kernel, jobs=jobs, other=other, groups=groups, own=own),
            out_shape=piece,
            in_specs=[anywhere] + [vmem] * 5,
            out_specs=vmem,
            scratch_shapes=[pltpu.VMEM((4, PACK, PIX), jnp.float32)],
            compiler_params=pltpu.CompilerParams(vmem_limit_bytes=8 * MIB),
            cost_estimate=pl.CostEstimate(flops=10**10, bytes_accessed=MIB, transcendentals=0),
        )(after, held_acc, ids_rows, *tables)

    met = {half: [], 0: []}
    done = ids_rows
    for first in (half, 0):
        for nears_here in ((3, 2), (1, 0)):
            jobs = tuple((near, first) for near in nears_here)
            send = transform(done, jobs, 1)
            got = swap(send, "grp", 1)
            keep = transform(send, jobs, 0)
            for k, near in enumerate(nears_here):
                span = slice(k * half, (k + 1) * half)
                part = keep[span].astype(jnp.float32) + got[span].astype(jnp.float32)
                part = part.astype(jnp.bfloat16)
                met[first].append(hop(part, near, groups) if near else part)
            done = part
    def regroup(after, first):
        return pl.pallas_call(
            functools.partial(regroup_kernel, first=first),
            out_shape=pltpu.VMEM((spans, fresh_count, 2, PIX), jnp.bfloat16),
            in_specs=[anywhere, hbm],
            out_specs=vmem,
            scratch_shapes=[pltpu.SemaphoreType.DMA((spans,))],
            compiler_params=pltpu.CompilerParams(vmem_limit_bytes=8 * MIB),
            cost_estimate=pl.CostEstimate(flops=10**8, bytes_accessed=MIB, transcendentals=0),
        )(after, block)

    fresh = []
    pieces = [None] * fars
    for first in (half, 0):
        totals = pl.pallas_call(
            functools.partial(totals_kernel, parts=nears),
            out_shape=[jax.ShapeDtypeStruct((block_rows, PIX), jnp.bfloat16)] * half,
            in_specs=[anywhere] + [vmem] * nears,
            out_specs=[vmem] * half,
            compiler_params=pltpu.CompilerParams(vmem_limit_bytes=8 * MIB),
        )(done, *met[first])
        for r, total in enumerate(totals):
            far = first + r
            pieces[far] = swap(total, "dp", far << 1) if far else total
        done = regroup(totals[0], len(fresh) * spans)
        fresh.append(done)
    summed = pl.pallas_call(
        added_kernel,
        out_shape=jax.ShapeDtypeStruct((block_rows, PIX), jnp.bfloat16),
        in_specs=[anywhere] + [vmem] * fars,
        out_specs=vmem,
        compiler_params=pltpu.CompilerParams(vmem_limit_bytes=8 * MIB),
    )(done, *put(pltpu.VMEM, *pieces))
    final_tables = jnp.asarray(expand_table()), jnp.asarray(filter_table())
    spread_scratch = [
        pltpu.VMEM((TILE * BAND + BAND, PIX), jnp.float32),
        pltpu.VMEM(((BAND + 1) * TILE, PIX), jnp.float32),
    ]
    averages, rounded = pl.pallas_call(
        functools.partial(averages_kernel, own=own, parts=fars),
        out_shape=(
            jax.ShapeDtypeStruct((own, 2, flat), jnp.float32),
            jax.ShapeDtypeStruct((TILE, 2 * flat), jnp.bfloat16),
        ),
        in_specs=[vmem] * (fars + 2),
        out_specs=(vmem, vmem),
        scratch_shapes=spread_scratch,
        compiler_params=pltpu.CompilerParams(vmem_limit_bytes=8 * MIB),
    )(*put(pltpu.VMEM, *pieces), *final_tables)

    def references(after, piece):
        return pl.pallas_call(
            functools.partial(references_kernel, own=own),
            out_shape=jax.ShapeDtypeStruct((TILE, 2 * flat), jnp.bfloat16),
            in_specs=[anywhere] + [vmem] * 3,
            out_specs=vmem,
            scratch_shapes=spread_scratch,
            compiler_params=pltpu.CompilerParams(vmem_limit_bytes=8 * MIB),
            cost_estimate=pl.CostEstimate(flops=10**10, bytes_accessed=MIB, transcendentals=0),
        )(after, *put(pltpu.VMEM, piece), *final_tables)

    held = [rounded, references(rounded, swap(summed, "grp", 1))]
    for k in range(2, groups, 2):
        across = swap(summed, "grp", k)
        held.append(references(held[-1], across))
        held.append(references(held[-1], swap(across, "grp", 1)))
    fresh = [f.reshape(spans, 2 * fresh_count, PIX) for f in fresh]
    scores = pl.pallas_call(
        functools.partial(scores_kernel, own=own, groups=groups),
        out_shape=jax.ShapeDtypeStruct((own * groups, fresh_count), jnp.float32),
        in_specs=[vmem] * (groups + len(fresh)),
        out_specs=vmem,
        scratch_shapes=[pltpu.VMEM((2 * fresh_count + TILE, PIX), jnp.float32)],
        compiler_params=pltpu.CompilerParams(vmem_limit_bytes=16 * MIB),
    )(*put(pltpu.VMEM, *held, *fresh))
    return averages, scores


def solution(mesh):
    placed = (
        P(("dp", "grp"), None, None),
        P(("dp", "grp"), None),
        P(("dp", "grp")),
        P("grp", None, None),
    )
    return jax.shard_map(
        body,
        mesh=mesh,
        in_specs=placed,
        out_specs=(P(("dp", "grp"), None, None), P("dp", "grp")),
        check_vma=False,
    )
```

```python
import functools
import math

import jax
import jax.numpy as jnp
import ml_dtypes
import numpy as np
from jax import lax
from jax.experimental import pallas as pl
from jax.experimental.pallas import tpu as pltpu
from jax.sharding import PartitionSpec as P

PIX = 128
BAND = 64
CLASSES = 256
HALF = BAND // 2
RIDGE = 4.0
REACH = 16
SLAB = PIX + 2 * REACH
TILE = 8
PACK = 16
ROWS = BAND + PACK
DIGITS = 4
CHUNK = 32
RING = 6
UNROLL = 32
MIB = 1 << 20


def basis():
    position = np.arange(PIX)
    freq = np.concatenate([np.arange(HALF + 1), np.arange(1, HALF + 1)])
    angle = (position[:, None] * freq[None, :] % PIX) * (2.0 * math.pi / PIX)
    is_cos = np.arange(BAND + 1) <= HALF
    table = np.where(is_cos[None, :], np.cos(angle), np.sin(angle)) / math.sqrt(PIX)
    return table.astype(np.float32).astype(ml_dtypes.bfloat16)


def column_table():
    table = basis()
    out = np.zeros((2 * PIX, PIX), ml_dtypes.bfloat16)
    for side in range(2):
        out[side * PIX : (side + 1) * PIX, side * BAND : (side + 1) * BAND] = table[:, :BAND]
    return out


def last_table(pairs):
    table = basis()
    out = np.zeros((PACK, pairs, 2 * PIX), ml_dtypes.bfloat16)
    for j in range(pairs):
        for side in range(2):
            out[j + side * pairs, j, side * PIX : (side + 1) * PIX] = table[:, BAND]
    return out.reshape(PACK, -1)


def row_table():
    out = np.zeros((ROWS, PIX), ml_dtypes.bfloat16)
    out[: BAND + 1] = basis().T
    return out


def expand_table():
    out = np.zeros((PIX, 2 * PIX), ml_dtypes.bfloat16)
    for at in range(BAND):
        k = at - HALF
        for copy in range(2):
            out[abs(k), copy * BAND + at] = 1.0
            if k:
                row = BAND if abs(k) == HALF else HALF + abs(k)
                out[row, PIX + copy * BAND + at] = math.copysign(1.0, k)
    return out


def filter_table():
    squared = (np.arange(BAND, dtype=np.float32) - HALF) ** 2
    radius = squared[:, None] + squared[None, :]
    return np.exp(-radius / (BAND * BAND / 2.0)).reshape(BAND // 2, 2 * BAND).astype(np.float32)


def owner_of(near, far, other, groups):
    dp, grp = lax.axis_index("dp"), lax.axis_index("grp")
    there_dp = dp ^ ((far << 1) | (near & 1))
    there_grp = grp ^ (((near >> 1) << 1) | other)
    return there_dp * groups + there_grp


def sums_kernel(
    class_ids, pixel_shifts, images, acc, held, ids, shifts, sems, small_sem
):
    chunks = images.shape[0] // CHUNK

    def fetch(k):
        span = pl.ds(pl.multiple_of(k * CHUNK, CHUNK), CHUNK)
        slot = lax.rem(k, RING)
        return pltpu.make_async_copy(images.at[span], held.at[slot], sems.at[slot])

    small = [
        pltpu.make_async_copy(class_ids, ids, small_sem.at[0]),
        pltpu.make_async_copy(pixel_shifts, shifts, small_sem.at[1]),
    ]
    for copy in small:
        copy.start()
    for k in range(min(RING, chunks)):
        fetch(k).start()
    acc[...] = jnp.zeros_like(acc)
    for copy in small:
        copy.wait()

    def add_chunk(k, _):
        fetch(k).wait()
        slot = lax.rem(k, RING)

        def add_some(s, _):
            for u in range(UNROLL):
                i = k * CHUNK + s * UNROLL + u
                dx = shifts[0, i]
                at = ids[i] * SLAB + REACH + shifts[1, i]
                turned = pltpu.roll(
                    held[slot, s * UNROLL + u].astype(jnp.float32), jnp.where(dx < 0, dx + PIX, dx), 1
                )
                acc[pl.ds(at, PIX), :] = acc[pl.ds(at, PIX), :] + turned
            return 0

        lax.fori_loop(0, CHUNK // UNROLL, add_some, 0)

        @pl.when(k + RING < chunks)
        def _():
            fetch(k + RING).start()

        return 0

    lax.fori_loop(0, chunks, add_chunk, 0)


def transform_kernel(
    _, acc, ids_rows, col, row, last, out, edges, *, jobs, other, groups, own
):
    pairs = own // 2
    count = out.shape[0]
    half = count // len(jobs)
    together = 4 if count % 4 == 0 else 1
    lane = lax.broadcasted_iota(jnp.int32, (TILE, ROWS), 1)
    sub = lax.broadcasted_iota(jnp.int32, (TILE, PIX), 0)
    edges[...] = jnp.zeros_like(edges)

    def folded(c):
        at = pl.multiple_of(c * SLAB, TILE)
        head = acc[pl.ds(at + REACH, REACH), :] + acc[pl.ds(at + PIX + REACH, REACH), :]
        mid = acc[pl.ds(at + 2 * REACH, PIX - 2 * REACH), :]
        tail = acc[pl.ds(at + PIX, REACH), :] + acc[pl.ds(at, REACH), :]
        return jnp.concatenate([head, mid, tail], axis=0).astype(jnp.bfloat16)

    def transform(far, edge):
        near, first = jobs[-1]
        which = lax.div(far, half)
        for k, job in enumerate(jobs[:-1]):
            near = jnp.where(which == k, job[0], near)
            first = jnp.where(which == k, job[1], first)
        owner = owner_of(near, first + lax.rem(far, half), other, groups)
        wide = jnp.concatenate(
            [folded(owner * own + j + side * pairs) for j in range(pairs) for side in range(2)], axis=1
        )
        part = jnp.dot(row[...], wide, preferred_element_type=jnp.float32).astype(jnp.bfloat16)
        ends = lax.dot_general(
            last[...], part, (((1,), (1,)), ((), ())), preferred_element_type=jnp.float32
        )
        full = jnp.dot(
            jnp.concatenate(
                [part[:, 2 * PIX * j : 2 * PIX * (j + 1)] for j in range(pairs)], axis=0
            ),
            col[...],
            preferred_element_type=jnp.float32,
        )
        for j in range(pairs):
            at = j * ROWS
            out[far, j * BAND : (j + 1) * BAND, :] = full[at : at + BAND].astype(jnp.bfloat16)
            edge[j : j + 1, :] = full[at + BAND : at + BAND + 1]
        hits = jnp.zeros((TILE, PIX), jnp.float32)
        for r in range(ids_rows.shape[0]):
            hits += (ids_rows[r : r + 1, :] == owner * own + sub).astype(jnp.float32)
        rest = jnp.sum(hits, axis=1, keepdims=True)
        ends = ends[:TILE]
        for d in range(DIGITS):
            upper = jnp.floor(rest * 0.125) if d < DIGITS - 1 else jnp.zeros_like(rest)
            ends = jnp.where(lane == BAND + 1 + d, rest - 8.0 * upper, ends)
            rest = upper
        edge[TILE:, :ROWS] = ends
        out[far, pairs * BAND :, :] = edge[...].astype(jnp.bfloat16)

    def some(n, _):
        for k in range(together):
            transform(n * together + k, edges.at[k])
        return 0

    lax.fori_loop(0, count // together, some, 0)


def regroup_kernel(_, block, fresh, sems, *, first):
    copies = [
        pltpu.make_async_copy(
            block.at[:, :, pl.ds((first + f) * PIX, PIX)], fresh.at[f], sems.at[f]
        )
        for f in range(fresh.shape[0])
    ]
    for copy in copies:
        copy.start()
    for copy in copies:
        copy.wait()


def totals_kernel(_, *refs, parts):
    for r, out in enumerate(refs[parts:]):
        total = refs[0][r].astype(jnp.float32)
        for ref in refs[1:parts]:
            total += ref[r].astype(jnp.float32)
        out[...] = total.astype(jnp.bfloat16)


def added(pieces):
    total = pieces[0][...].astype(jnp.float32)
    for piece in pieces[1:]:
        total += piece[...].astype(jnp.float32)
    return total


def added_kernel(_, *refs):
    refs[-1][...] = added(refs[:-1]).astype(jnp.bfloat16)


def averages_kernel(*refs, own, parts):
    pieces, (expand, taper, out, rounded, wide, rows) = refs[:parts], refs[parts:]

    def emit(u, part, value):
        out[:, part, u * PIX : (u + 1) * PIX] = value[:own]
        at = part * BAND * BAND + u * PIX
        rounded[:, at : at + PIX] = value

    spread_out(added(pieces), 3, expand, taper, wide, rows, own, emit)


def references_kernel(*refs, own):
    _, piece, expand, taper, rounded, wide, rows = refs

    def emit(u, part, value):
        at = part * BAND * BAND + u * PIX
        rounded[:, at : at + PIX] = value

    spread_out(piece[...].astype(jnp.float32), 1, expand, taper, wide, rows, own, emit)


def spread_out(total, pieces, expand, taper, wide, rows, own, emit):
    pairs = own // 2
    main, ends = total[: pairs * BAND], total[pairs * BAND :]
    if own < TILE:
        wide[...] = jnp.zeros_like(wide)
    wide[: pairs * BAND, :] = main
    wide[pairs * BAND : 2 * pairs * BAND, :] = pltpu.roll(main, BAND, 1)
    extra = ends[TILE:]
    lane = lax.broadcasted_iota(jnp.int32, (TILE, PIX), 1)
    for t in range(BAND + 1):
        if t < BAND:
            line = wide[pl.ds(t, TILE, stride=BAND), :]
        else:
            edge = ends[:pairs]
            line = jnp.concatenate([edge, pltpu.roll(ends[:TILE], BAND, 1)[:pairs]], axis=0)
            if own < TILE:
                line = jnp.concatenate([line, jnp.zeros((TILE - own, PIX), jnp.float32)], axis=0)
        line = jnp.where(
            lane < BAND, line, jnp.where(lane == BAND, extra[:, t : t + 1], 0.0)
        )
        rows[t * TILE : (t + 1) * TILE, :] = line
    spread = None
    rest = rows[...]
    for k in range(pieces):
        here = rest.astype(jnp.bfloat16)
        rest = rest - here.astype(jnp.float32) if k + 1 < pieces else None
        term = jnp.dot(here, expand[...], preferred_element_type=jnp.float32)
        spread = term if spread is None else spread + term

    def cos_part(t):
        return spread[t * TILE : (t + 1) * TILE, :PIX]

    def sin_part(t):
        return spread[t * TILE : (t + 1) * TILE, PIX:]

    members = jnp.zeros((TILE, 1), jnp.float32)
    for d in range(DIGITS):
        members += extra[:, BAND + 1 + d : BAND + 2 + d] * float(8**d)
    weight = members + RIDGE

    def at_frequency(k):
        c = abs(k)
        if k == 0:
            return cos_part(0), -sin_part(0)
        s = BAND if c == HALF else HALF + c
        if k > 0:
            return cos_part(c) - sin_part(s), -(cos_part(s) + sin_part(c))
        return cos_part(c) + sin_part(s), cos_part(s) - sin_part(c)

    for u in range(BAND // 2):
        even, odd = at_frequency(2 * u - HALF), at_frequency(2 * u + 1 - HALF)
        for part in range(2):
            value = jnp.where(lane < BAND, even[part], odd[part]) * taper[u : u + 1, :] / weight
            emit(u, part, value)


def scores_kernel(*refs, own, groups):
    pieces, fresh, (out, sums) = refs[:groups], refs[groups:-2], refs[-2:]
    each = fresh[0].shape[0]
    spans = len(fresh) * each
    classes = own * groups
    held = jnp.concatenate([piece[:own] for piece in pieces], axis=0).astype(jnp.bfloat16)
    both = jnp.concatenate([held[:, : spans * PIX], held[:, spans * PIX :]], axis=0)
    total = None
    for f in range(0, spans, 2):
        here = jnp.concatenate([fresh[g // each][g % each] for g in (f, f + 1)], axis=1)
        term = lax.dot_general(
            here,
            both[:, f * PIX : (f + 2) * PIX],
            (((1,), (1,)), ((), ())),
            preferred_element_type=jnp.float32,
        )
        total = term if total is None else total + term
    sums[: total.shape[0], : 2 * classes] = total
    count = out.shape[1]
    inner = sums[pl.ds(0, count, stride=2), :] + pltpu.roll(
        sums[pl.ds(1, count, stride=2), :], PIX - classes, 1
    )
    energy = jnp.sum(jnp.square(held.astype(jnp.float32)), axis=1, keepdims=True)
    result = (inner.T[:classes] - 0.5 * energy) / BAND
    for k in range(groups):
        at = (lax.axis_index("grp") ^ k) * own
        if own % TILE == 0:
            out[pl.ds(pl.multiple_of(at, TILE), own), :] = result[k * own : (k + 1) * own]
        else:
            for j in range(own):
                out[pl.ds(at + j, 1), :] = result[k * own + j : k * own + j + 1]


def swap(array, axis, flip):
    size = lax.axis_size(axis)
    return lax.ppermute(array, axis, [(i, i ^ flip) for i in range(size)])


def hop(array, near, groups):
    both = lax.axis_size("dp") * groups
    return lax.ppermute(
        array,
        ("dp", "grp"),
        [(i, i ^ ((near & 1) * groups | (near >> 1) * 2)) for i in range(both)],
    )


def body(images, shifts, class_ids, next_block):
    dp_count, groups = lax.axis_size("dp"), lax.axis_size("grp")
    own = CLASSES // (dp_count * groups)
    pairs = own // 2
    count = images.shape[0]
    nears, fars = groups, dp_count // 2
    block_rows = pairs * BAND + PACK
    vmem = pl.BlockSpec(memory_space=pltpu.VMEM)
    hbm = pl.BlockSpec(memory_space=pltpu.HBM)
    anywhere = pl.BlockSpec(memory_space=pl.ANY)
    flat = BAND * BAND
    spans = flat // PIX // 2
    fresh_count = next_block.shape[0]

    def put(space, *arrays):
        return [pltpu.with_memory_space_constraint(a, space) for a in arrays]

    acc = pl.pallas_call(
        sums_kernel,
        out_shape=pltpu.VMEM((CLASSES * SLAB, PIX), jnp.float32),
        in_specs=[hbm] * 3,
        out_specs=vmem,
        scratch_shapes=[
            pltpu.VMEM((RING, CHUNK, PIX, PIX), jnp.bfloat16),
            pltpu.SMEM((count,), jnp.int32),
            pltpu.SMEM((2, count), jnp.int32),
            pltpu.SemaphoreType.DMA((RING,)),
            pltpu.SemaphoreType.DMA((2,)),
        ],
        compiler_params=pltpu.CompilerParams(vmem_limit_bytes=10 * MIB),
    )(*put(pltpu.HBM, class_ids, shifts.T, images))
    half = fars // 2
    piece = jax.ShapeDtypeStruct((2 * half, block_rows, PIX), jnp.bfloat16)
    ids_rows = class_ids.reshape(count // PIX, PIX)
    tables = [jnp.asarray(t) for t in (column_table(), row_table(), last_table(pairs))]

    (block,) = put(pltpu.HBM, next_block)
    (held_acc,) = put(pltpu.VMEM, acc)

    def transform(after, jobs, other):
        return pl.pallas_call(
            functools.partial(transform_kernel, jobs=jobs, other=other, groups=groups, own=own),
            out_shape=piece,
            in_specs=[anywhere] + [vmem] * 5,
            out_specs=vmem,
            scratch_shapes=[pltpu.VMEM((4, PACK, PIX), jnp.float32)],
            compiler_params=pltpu.CompilerParams(vmem_limit_bytes=8 * MIB),
            cost_estimate=pl.CostEstimate(flops=10**10, bytes_accessed=MIB, transcendentals=0),
        )(after, held_acc, ids_rows, *tables)

    met = {half: [], 0: []}
    done = ids_rows
    for first in (half, 0):
        for nears_here in ((3, 2), (1, 0)):
            jobs = tuple((near, first) for near in nears_here)
            send = transform(done, jobs, 1)
            got = swap(send, "grp", 1)
            keep = transform(send, jobs, 0)
            for k, near in enumerate(nears_here):
                span = slice(k * half, (k + 1) * half)
                part = keep[span].astype(jnp.float32) + got[span].astype(jnp.float32)
                part = part.astype(jnp.bfloat16)
                met[first].append(hop(part, near, groups) if near else part)
            done = part
    def regroup(after, first):
        return pl.pallas_call(
            functools.partial(regroup_kernel, first=first),
            out_shape=pltpu.VMEM((spans, fresh_count, 2, PIX), jnp.bfloat16),
            in_specs=[anywhere, hbm],
            out_specs=vmem,
            scratch_shapes=[pltpu.SemaphoreType.DMA((spans,))],
            compiler_params=pltpu.CompilerParams(vmem_limit_bytes=8 * MIB),
            cost_estimate=pl.CostEstimate(flops=10**8, bytes_accessed=MIB, transcendentals=0),
        )(after, block)

    fresh = []
    pieces = [None] * fars
    for first in (half, 0):
        totals = pl.pallas_call(
            functools.partial(totals_kernel, parts=nears),
            out_shape=[jax.ShapeDtypeStruct((block_rows, PIX), jnp.bfloat16)] * half,
            in_specs=[anywhere] + [vmem] * nears,
            out_specs=[vmem] * half,
            compiler_params=pltpu.CompilerParams(vmem_limit_bytes=8 * MIB),
        )(done, *met[first])
        for r, total in enumerate(totals):
            far = first + r
            pieces[far] = swap(total, "dp", far << 1) if far else total
        done = regroup(totals[0], len(fresh) * spans)
        fresh.append(done)
    summed = pl.pallas_call(
        added_kernel,
        out_shape=jax.ShapeDtypeStruct((block_rows, PIX), jnp.bfloat16),
        in_specs=[anywhere] + [vmem] * fars,
        out_specs=vmem,
        compiler_params=pltpu.CompilerParams(vmem_limit_bytes=8 * MIB),
    )(done, *put(pltpu.VMEM, *pieces))
    final_tables = jnp.asarray(expand_table()), jnp.asarray(filter_table())
    spread_scratch = [
        pltpu.VMEM((TILE * BAND + BAND, PIX), jnp.float32),
        pltpu.VMEM(((BAND + 1) * TILE, PIX), jnp.float32),
    ]
    averages, rounded = pl.pallas_call(
        functools.partial(averages_kernel, own=own, parts=fars),
        out_shape=(
            jax.ShapeDtypeStruct((own, 2, flat), jnp.float32),
            jax.ShapeDtypeStruct((TILE, 2 * flat), jnp.float32),
        ),
        in_specs=[vmem] * (fars + 2),
        out_specs=(vmem, vmem),
        scratch_shapes=spread_scratch,
        compiler_params=pltpu.CompilerParams(vmem_limit_bytes=8 * MIB),
    )(*put(pltpu.VMEM, *pieces), *final_tables)

    def references(after, piece):
        return pl.pallas_call(
            functools.partial(references_kernel, own=own),
            out_shape=jax.ShapeDtypeStruct((TILE, 2 * flat), jnp.float32),
            in_specs=[anywhere] + [vmem] * 3,
            out_specs=vmem,
            scratch_shapes=spread_scratch,
            compiler_params=pltpu.CompilerParams(vmem_limit_bytes=8 * MIB),
            cost_estimate=pl.CostEstimate(flops=10**10, bytes_accessed=MIB, transcendentals=0),
        )(after, *put(pltpu.VMEM, piece), *final_tables)

    held = [rounded, references(rounded, swap(summed, "grp", 1))]
    for k in range(2, groups, 2):
        across = swap(summed, "grp", k)
        held.append(references(held[-1], across))
        held.append(references(held[-1], swap(across, "grp", 1)))
    fresh = [f.reshape(spans, 2 * fresh_count, PIX) for f in fresh]
    scores = pl.pallas_call(
        functools.partial(scores_kernel, own=own, groups=groups),
        out_shape=jax.ShapeDtypeStruct((own * groups, fresh_count), jnp.float32),
        in_specs=[vmem] * (groups + len(fresh)),
        out_specs=vmem,
        scratch_shapes=[pltpu.VMEM((2 * fresh_count + TILE, PIX), jnp.float32)],
        compiler_params=pltpu.CompilerParams(vmem_limit_bytes=16 * MIB),
    )(*put(pltpu.VMEM, *held, *fresh))
    return averages, scores


def solution(mesh):
    placed = (
        P(("dp", "grp"), None, None),
        P(("dp", "grp"), None),
        P(("dp", "grp")),
        P("grp", None, None),
    )
    return jax.shard_map(
        body,
        mesh=mesh,
        in_specs=placed,
        out_specs=(P(("dp", "grp"), None, None), P("dp", "grp")),
        check_vma=False,
    )
```
